32 devices in a mesh: stn: 16 (over z, y, x), chan: 2 (over core).
Axes of the slice: x: 2, y: 2, z: 4, core: 2. Of those that a mesh axis runs over, the one named last changes fastest.
Arguments:
- voltages: bfloat16 [128, 4, 64, 128], P('stn', 'chan'), may hold values from -12 to 12
- response: bfloat16 [128, 4, 64, 128], P('stn', 'chan'), may hold values from -48 to 48
- start_gains: float32 [128, 128], replicated, may hold values from 0.5 to 1.5
- step_sizes: float32 [64], replicated, may hold values from 0.2 to 0.8
- station_ids: int32 [128], P('stn'), may hold values from 0 to 127, each once
- baseline_flags: int32 [128, 128], replicated, may hold values 0 or 1
Outputs:
- calibrated: float32 [128, 128], P('stn')
- descent: float32 [128, 128], P('stn')
The draws below stay inside these ranges and needn't reach their ends.
Inputs may be any that keep to these rules, and one draw needn't show every extreme that they name: `station_ids`: each station number appears once. `baseline_flags`: 1 keeps a baseline, 0 flags it.
All inputs are finite; a program needn't handle non-finite values.
Results may differ from the reference program's by a relative error of at most 0.0003.
Values may be sent and summed in bfloat16 or wider, within the bound.
A program may use at most 64 MiB of HBM per device.

```python
import math
import jax
import jax.numpy as jnp
from jax import lax

S = 128
K = 64
NV = 64
TIMES = 64
F = 4
ITERS = 2


def draw_response(key, part):
    keys = jax.random.split(key, 3)
    station_pos = jnp.arange(S, dtype=jnp.float32).reshape(S, 1, 1, 1) / (S - 1)
    station_scale = jnp.exp(jnp.log(3.0) * (station_pos + jax.random.uniform(keys[1], (S, 1, 1, 1), jnp.float32, -0.5, 0.5)))
    direction_scale = jnp.exp(jax.random.uniform(keys[2], (K,), jnp.float32, jnp.log(0.3), jnp.log(3.0)))
    direction_scale = jnp.concatenate([direction_scale, direction_scale]).reshape(1, 1, 1, 2 * K)
    base = jnp.clip(jax.random.normal(keys[0], (S, F, TIMES, 2 * K), jnp.float32), -3.0, 3.0)
    return (base * station_scale * direction_scale).astype(jnp.bfloat16)


def plant(result, rng, smallest, top_value):
    dims = result.shape
    index_at = [jax.random.randint(jax.random.fold_in(rng, axis), (), 0, dims[axis]) for axis in range(len(dims))]
    result = result.at[tuple(index_at)].set(smallest)
    longest = dims.index(max(dims))
    index_at[longest] = (index_at[longest] + 1) % dims[longest]
    return result.at[tuple(index_at)].set(top_value)


def block_scale(own_key, extent, cuts, least, largest):
    factor_of = 1.0
    for dim, blocks in cuts:
        heights = jax.random.uniform(jax.random.fold_in(jax.random.fold_in(own_key, 6), dim), (blocks,), jnp.float32, least / len(cuts), largest / len(cuts))
        factor_of = factor_of * jnp.repeat(jnp.exp(heights), extent[dim] // blocks).reshape((-1,) + (1,) * (len(extent) - 1 - dim))
    return factor_of


def normal_values(rng, shape, deviation, limit, cuts=(), held_as=jnp.bfloat16):
    gain = block_scale(rng, shape, cuts, -0.22, 0.18) if cuts else 1.0
    drawn = jax.random.normal(rng, shape, jnp.float32) * deviation * gain
    return jnp.minimum(jnp.maximum(drawn, -limit), limit).astype(held_as)


def setup_inputs(seed: int = 0) -> dict:
    seeds = jax.random.split(jax.random.key(seed), 7)
    voltages = normal_values(seeds[0], (S, F, TIMES, 2 * NV), 3.0, 12.0, ((0, 16), (1, 2)))
    response = draw_response(jax.random.fold_in(seeds[6], 71), 0)
    start_gains = jnp.clip(1.0 + 0.1 * jax.random.normal(seeds[2], (S, 2 * K), jnp.float32), 0.5, 1.5)
    step_sizes = jnp.clip(jnp.exp(jax.random.uniform(seeds[3], (K,), jnp.float32, math.log(0.2), math.log(0.8))), 0.2, 0.8)
    station_ids = jax.random.permutation(seeds[4], S).astype(jnp.int32)
    baseline_flags = plant((jax.random.randint(seeds[5], (S, S), 0, 8) < 7).astype(jnp.int32), jax.random.fold_in(seeds[5], 1), 0, 1)
    return dict(voltages=voltages, response=response, start_gains=start_gains, step_sizes=step_sizes, station_ids=station_ids, baseline_flags=baseline_flags)


def rotate(values, middle):
    return jnp.concatenate([-values[..., middle:], values[..., :middle]], axis=-1)

def correlate(mine, middle):
    highest = lax.Precision.HIGHEST
    real_part = jnp.einsum('tpc,tqc->tpq', mine, mine, precision=highest)
    imag_part = jnp.einsum('tpc,tqc->tpq', mine, rotate(mine, middle), precision=highest)
    return (real_part / middle, imag_part / middle)

def reference(voltages, response, start_gains, step_sizes, station_ids, baseline_flags):
    highest = lax.Precision.HIGHEST
    samples = F * TIMES
    block = 8
    count = samples // block
    volt_blocks = voltages.astype(jnp.float32).reshape(S, samples, 2 * NV).transpose(1, 0, 2).reshape(count, block, S, 2 * NV)
    resp_blocks = response.astype(jnp.float32).reshape(S, samples, 2 * K).transpose(1, 0, 2).reshape(count, block, S, 2 * K)
    flag_float = baseline_flags.astype(jnp.float32)
    picked = jnp.take(jnp.take(flag_float, station_ids, axis=0), station_ids, axis=1)
    weight = picked * picked.T * (1.0 - jnp.eye(S, dtype=jnp.float32))
    step_both = jnp.concatenate([step_sizes, step_sizes])
    current = start_gains
    descent = jnp.zeros_like(start_gains)
    for iteration in range(ITERS):
        gain_real = current[None, :, :K]
        gain_imag = current[None, :, K:]

        def one_block(total, pieces):
            volts, resp = pieces
            resp_real = resp[..., :K]
            resp_imag = resp[..., K:]
            applied = jnp.concatenate([gain_real * resp_real - gain_imag * resp_imag, gain_real * resp_imag + gain_imag * resp_real], axis=-1).astype(jnp.bfloat16)
            applied_float = lax.optimization_barrier(applied).astype(jnp.float32)
            seen_real, seen_imag = correlate(volts, NV)
            pred_real, pred_imag = correlate(applied_float, K)
            resid_real = (weight[None] * (seen_real - pred_real)).astype(jnp.bfloat16)
            resid_imag = (weight[None] * (seen_imag - pred_imag)).astype(jnp.bfloat16)
            resid_real = lax.optimization_barrier(resid_real).astype(jnp.float32)
            resid_imag = lax.optimization_barrier(resid_imag).astype(jnp.float32)
            hidden = jnp.einsum('tpq,tqc->tpc', resid_real, applied_float, precision=highest)
            hidden = hidden + jnp.einsum('tpq,tqc->tpc', resid_imag, rotate(applied_float, K), precision=highest)
            energy_real = lax.optimization_barrier(jnp.sum(resp_real * hidden[..., :K] + resp_imag * hidden[..., K:], axis=0))
            energy_imag = lax.optimization_barrier(jnp.sum(resp_real * hidden[..., K:] - resp_imag * hidden[..., :K], axis=0))
            return (total + jnp.concatenate([energy_real, energy_imag], axis=-1), None)
        energy, unused = lax.scan(one_block, jnp.zeros((S, 2 * K), jnp.float32), (volt_blocks, resp_blocks))
        gradient = -(2.0 / K) * energy
        spread = jnp.sqrt(jnp.sum(gradient * gradient) / (S * K) + 1e-06)
        descent = gradient / spread
        current = current - step_both[None, :] * descent
    return (current, descent)
```

```python
import functools

import jax
import jax.numpy as jnp
from jax import lax
from jax.experimental import pallas as pl
from jax.experimental.pallas import tpu as pltpu
from jax.sharding import PartitionSpec as P

ITERS = 2
MESH = pl.DeviceIdType.MESH
IDS, RESP, VOLT, SUMS, GATHER = 0, 1, 2, 3, 3 + ITERS
GROUPS = 3 + 2 * ITERS


def dot_last(left, right):
    return lax.dot_general(left, right, (((1,), (1,)), ((), ())), preferred_element_type=jnp.float32)


def dot(left, right):
    return lax.dot_general(left, right, (((1,), (0,)), ((), ())), preferred_element_type=jnp.float32)


def kernel(
    n, nchan, stations, samples,
    volt_any, resp_any, gains_any, steps_ref, ids_ref, flags_any,
    calibrated_ref, descent_ref,
    volt_in, resp_in, gains, flags, wide_volt, wide_resp,
    volt_send, resp_send, volt_recv, resp_recv, id_rows,
    weight, a_float, a_swap, applied, observed, diff,
    energy_out, sums, gathered, current,
    in_sem, send_sem, recv_sem,
):
    everyone = n * stations
    devices = n * nchan
    spd = samples // n
    rows = stations // nchan
    width = volt_in.shape[2]
    half = width // 2
    stn = lax.axis_index("stn")
    chan = lax.axis_index("chan")
    me = stn * nchan + chan

    def place(d):
        return {"stn": d // nchan, "chan": lax.rem(d, nchan)}

    loads = [
        pltpu.make_async_copy(src, dst, in_sem.at[i])
        for i, (src, dst) in enumerate(
            ((resp_any, resp_in), (volt_any, volt_in), (flags_any, flags), (gains_any, gains))
        )
    ]
    for load in loads:
        load.start()

    barrier = pltpu.get_barrier_semaphore()

    def greet(k, carry):
        pl.semaphore_signal(barrier, inc=1, device_id=place(lax.rem(me + k, devices)), device_id_type=MESH)
        return carry

    lax.fori_loop(1, devices, greet, 0)

    def wait_all(buffer, count, sem):
        part = buffer.at[pl.ds(0, count)]
        pltpu.make_async_copy(part, part, sem).wait()

    lane = lax.broadcasted_iota(jnp.int32, (1, everyone), 1)
    own_row = jnp.zeros((1, everyone), jnp.int32)
    for j in range(stations):
        own_row = jnp.where(lane == stn * stations + j, ids_ref[j], own_row)
    id_rows[stn] = own_row

    loads[0].wait()
    wide_resp[...] = resp_in[...].astype(jnp.float32).reshape(stations * samples, width)

    def pack(wide, send, dst):
        for pair in range(spd // 2):
            first = dst * spd + 2 * pair
            both = jnp.concatenate(
                [wide[pl.ds(first + j, stations, stride=samples), :] for j in range(2)], axis=0
            )
            send[dst, pl.ds(2 * pair * stations, 2 * stations), :] = both.astype(jnp.bfloat16)

    def to_stn(src, dst_ref, group, dst):
        pltpu.make_async_remote_copy(
            src_ref=src, dst_ref=dst_ref.at[stn], send_sem=send_sem.at[group],
            recv_sem=recv_sem.at[group], device_id={"stn": dst}, device_id_type=MESH,
        ).start()

    pl.semaphore_wait(barrier, devices - 1)

    def send_resp(k, carry):
        dst = lax.rem(stn + k, n)
        to_stn(id_rows.at[stn], id_rows, IDS, dst)
        pack(wide_resp, resp_send, dst)
        to_stn(resp_send.at[dst], resp_recv, RESP, dst)
        return carry

    lax.fori_loop(1, n, send_resp, 0)
    loads[1].wait()
    wide_volt[...] = volt_in[...].astype(jnp.float32).reshape(stations * samples, width)

    def send_volt(k, carry):
        dst = lax.rem(stn + k, n)
        pack(wide_volt, volt_send, dst)
        to_stn(volt_send.at[dst], volt_recv, VOLT, dst)
        return carry

    lax.fori_loop(1, n, send_volt, 0)
    pack(wide_resp, resp_send, stn)
    resp_recv[stn] = resp_send[stn]
    pack(wide_volt, volt_send, stn)
    volt_recv[stn] = volt_send[stn]

    loads[2].wait()
    flag = flags[...].astype(jnp.float32)
    mutual = (flag * flag.T).astype(jnp.bfloat16)
    wait_all(id_rows, n - 1, recv_sem.at[IDS])
    all_ids = jnp.sum(id_rows[...], axis=0)
    row = lax.broadcasted_iota(jnp.int32, (everyone, everyone), 0)
    column = lax.broadcasted_iota(jnp.int32, (everyone, everyone), 1)
    one_hot = (row == all_ids).astype(jnp.float32).astype(jnp.bfloat16)
    picked = dot(mutual, one_hot).T.astype(jnp.bfloat16)
    weight[...] = jnp.where(row == column, 0.0, dot(picked, one_hot))

    def unpack(recv, pair):
        block = recv[:, pl.ds(2 * pair * stations, 2 * stations), :].astype(jnp.float32)
        block = block.reshape(n, 2, stations, width)
        return [block[:, j].reshape(everyone, width) for j in range(2)]

    sign = jnp.where(lax.broadcasted_iota(jnp.int32, (1, width), 1) < half, -1.0, 1.0)
    loads[3].wait()
    steps = steps_ref[...].reshape(1, half)
    steps = jnp.concatenate([steps, steps], axis=1)

    def predict(t, gain_both, gain_turn):
        a = a_float[t]
        turned = gain_both * a + gain_turn * a_swap[t]
        applied[t, pl.ds(0, everyone), :] = turned.astype(jnp.bfloat16)
        applied[t, pl.ds(everyone, everyone), :] = (sign * pltpu.roll(turned, half, 1)).astype(jnp.bfloat16)
        return dot_last(applied[t, pl.ds(0, everyone), :], applied[t])

    def gain_parts(gain):
        swapped = pltpu.roll(gain, half, 1)
        left = sign < 0.0
        return jnp.where(left, gain, swapped), jnp.where(left, -swapped, gain)

    wait_all(resp_recv, n - 1, recv_sem.at[RESP])
    gain_both, gain_turn = gain_parts(gains[...])
    for pair in range(spd // 2):
        for j, a in enumerate(unpack(resp_recv, pair)):
            t = 2 * pair + j
            a_float[t] = a
            a_swap[t] = pltpu.roll(a, half, 1)
            diff[t] = predict(t, gain_both, gain_turn)

    wait_all(volt_recv, n - 1, recv_sem.at[VOLT])
    for pair in range(spd // 2):
        for j, x in enumerate(unpack(volt_recv, pair)):
            t = 2 * pair + j
            mine = x.astype(jnp.bfloat16)
            both = jnp.concatenate([mine, (sign * pltpu.roll(x, half, 1)).astype(jnp.bfloat16)], axis=0)
            seen = dot_last(mine, both)
            observed[t] = seen
            diff[t] = seen - diff[t]

    for iteration in range(ITERS):
        if iteration > 0:
            gain_both, gain_turn = gain_parts(current[...])
            for t in range(spd):
                diff[t] = observed[t] - predict(t, gain_both, gain_turn)
        direct = jnp.zeros((everyone, width), jnp.float32)
        crossed = jnp.zeros((everyone, width), jnp.float32)
        for t in range(spd):
            residual = jnp.concatenate(
                [
                    (weight[...] * diff[t, :, pl.ds(0, everyone)]).astype(jnp.bfloat16),
                    (weight[...] * diff[t, :, pl.ds(everyone, everyone)]).astype(jnp.bfloat16),
                ],
                axis=1,
            )
            hidden = dot(residual, applied[t])
            direct = direct + a_float[t] * hidden
            crossed = crossed + a_swap[t] * hidden
        energy = jnp.where(
            sign < 0.0,
            direct + pltpu.roll(direct, half, 1),
            crossed - pltpu.roll(crossed, half, 1),
        )
        energy_out[iteration] = energy.reshape(devices, rows, width)
        sums[iteration, me] = energy_out[iteration, me]

        def send_sum(k, carry):
            d = lax.rem(me + k, devices)
            pltpu.make_async_remote_copy(
                src_ref=energy_out.at[iteration, d], dst_ref=sums.at[iteration, me],
                send_sem=send_sem.at[SUMS + iteration], recv_sem=recv_sem.at[SUMS + iteration],
                device_id=place(d), device_id_type=MESH,
            ).start()
            return carry

        lax.fori_loop(1, devices, send_sum, 0)
        wait_all(sums.at[iteration], devices - 1, recv_sem.at[SUMS + iteration])
        scale = -(2.0 / half) / half
        gathered[iteration, me] = scale * jnp.sum(sums[iteration], axis=0)

        def send_block(k, carry):
            d = lax.rem(me + k, devices)
            pltpu.make_async_remote_copy(
                src_ref=gathered.at[iteration, me], dst_ref=gathered.at[iteration, me],
                send_sem=send_sem.at[GATHER + iteration], recv_sem=recv_sem.at[GATHER + iteration],
                device_id=place(d), device_id_type=MESH,
            ).start()
            return carry

        lax.fori_loop(1, devices, send_block, 0)
        wait_all(gathered.at[iteration], devices - 1, recv_sem.at[GATHER + iteration])
        gradient = gathered[iteration].reshape(everyone, width)
        spread = jnp.sqrt(jnp.sum(gradient * gradient, keepdims=True) / (everyone * half) + 1e-06)
        descent = gradient / spread
        if iteration == 0:
            current[...] = gains[...] - steps * descent
        else:
            current[...] = current[...] - steps * descent
        if iteration == ITERS - 1:
            gains[...] = descent
            own = pl.ds(pl.multiple_of(stn * stations, stations), stations)
            calibrated_ref[...] = current[own, :]
            descent_ref[...] = gains[own, :]

    wait_all(id_rows, n - 1, send_sem.at[IDS])
    wait_all(resp_send, n - 1, send_sem.at[RESP])
    wait_all(volt_send, n - 1, send_sem.at[VOLT])
    for iteration in range(ITERS):
        wait_all(sums.at[iteration], devices - 1, send_sem.at[SUMS + iteration])
        wait_all(gathered.at[iteration], devices - 1, send_sem.at[GATHER + iteration])


def shards(n, nchan, voltages, response, start_gains, step_sizes, station_ids, baseline_flags):
    stations, width = voltages.shape[0], voltages.shape[3]
    samples = voltages.shape[1] * voltages.shape[2]
    everyone = stations * n
    devices = n * nchan
    spd = samples // n
    rows = stations // nchan
    f32, bf16 = jnp.float32, jnp.bfloat16
    anywhere = pl.BlockSpec(memory_space=pl.ANY)
    vmem = pl.BlockSpec(memory_space=pltpu.VMEM)
    block = (n, spd * stations, width)
    scratch = [
        ((stations, samples, width), bf16),
        ((stations, samples, width), bf16),
        ((everyone, width), f32),
        ((everyone, everyone), jnp.int32),
        ((stations * samples, width), f32),
        ((stations * samples, width), f32),
        (block, bf16),
        (block, bf16),
        (block, bf16),
        (block, bf16),
        ((n, 1, everyone), jnp.int32),
        ((everyone, everyone), f32),
        ((spd, everyone, width), f32),
        ((spd, everyone, width), f32),
        ((spd, 2 * everyone, width), bf16),
        ((spd, everyone, 2 * everyone), f32),
        ((spd, everyone, 2 * everyone), f32),
        ((ITERS, devices, rows, width), f32),
        ((ITERS, devices, rows, width), f32),
        ((ITERS, devices, rows, width), f32),
        ((everyone, width), f32),
    ]
    return pl.pallas_call(
        functools.partial(kernel, n, nchan, stations, samples),
        out_shape=[jax.ShapeDtypeStruct((stations, width), f32)] * 2,
        in_specs=[anywhere, anywhere, anywhere, vmem, pl.BlockSpec(memory_space=pltpu.SMEM), anywhere],
        out_specs=[vmem, vmem],
        scratch_shapes=[pltpu.VMEM(shape, dtype) for shape, dtype in scratch]
        + [pltpu.SemaphoreType.DMA((4,)), pltpu.SemaphoreType.DMA((GROUPS,)), pltpu.SemaphoreType.DMA((GROUPS,))],
        compiler_params=pltpu.CompilerParams(
            collective_id=0, has_side_effects=True, vmem_limit_bytes=48 * 1024 * 1024
        ),
    )(
        voltages.reshape(stations, samples, width),
        response.reshape(stations, samples, width),
        start_gains, step_sizes, station_ids, baseline_flags,
    )


def solution(mesh):
    placed = (P("stn", "chan", None, None), P("stn", "chan", None, None), P(), P(), P("stn"), P())
    return jax.shard_map(
        functools.partial(shards, mesh.shape["stn"], mesh.shape["chan"]),
        mesh=mesh,
        in_specs=placed,
        out_specs=(P("stn", None), P("stn", None)),
        check_vma=False,
    )
```

```python
import functools

import jax
import jax.numpy as jnp
from jax import lax
from jax.experimental import pallas as pl
from jax.experimental.pallas import tpu as pltpu
from jax.sharding import PartitionSpec as P

ITERS = 2
MESH = pl.DeviceIdType.MESH
IDS, RESP, VOLT, SUMS, GATHER = 0, 1, 2, 4, 4 + ITERS
NORM = GATHER + ITERS
GROUPS = NORM + 1


def dot_last(left, right):
    return lax.dot_general(left, right, (((1,), (1,)), ((), ())), preferred_element_type=jnp.float32)


def dot(left, right):
    return lax.dot_general(left, right, (((1,), (0,)), ((), ())), preferred_element_type=jnp.float32)


def kernel(
    n, nchan, stations, samples,
    volt_any, resp_any, gains_any, steps_any, ids_any, flags_any,
    calibrated_ref, descent_ref,
    volt_in, resp_in, gains, flags, wide_volt, wide_resp,
    volt_send, resp_send, volt_recv, resp_recv, id_rows,
    weight, a_float, a_swap, applied, observed, diff,
    energy_out, sums, gathered, norms, current, steps_ref, ids_ref,
    in_sem, send_sem, recv_sem,
):
    everyone = n * stations
    devices = n * nchan
    spd = samples // n
    rows = stations // nchan
    width = volt_in.shape[2]
    half = width // 2
    stn = lax.axis_index("stn")
    chan = lax.axis_index("chan")
    me = stn * nchan + chan

    def each(first, stop, body):
        if stop - first <= 16:
            for k in range(first, stop):
                body(k)
        else:
            lax.fori_loop(first, stop, lambda k, carry: (body(k), carry)[1], 0)

    def other_stations(body):
        each(1, n, lambda k: body(lax.rem(stn + k, n)))

    def other_devices(body):
        each(1, n, lambda k: [body(lax.rem(stn + k, n), lax.rem(chan + c, nchan)) for c in range(nchan)])
        for c in range(1, nchan):
            body(stn, lax.rem(chan + c, nchan))

    loads = [
        pltpu.make_async_copy(src, dst, in_sem.at[i])
        for i, (src, dst) in enumerate(
            (
                (ids_any, ids_ref), (resp_any, resp_in), (volt_any, volt_in),
                (flags_any, flags), (gains_any, gains), (steps_any, steps_ref),
            )
        )
    ]
    for load in loads:
        load.start()

    barrier = pltpu.get_barrier_semaphore()

    def greet(s, c):
        pl.semaphore_signal(barrier, inc=1, device_id={"stn": s, "chan": c}, device_id_type=MESH)

    other_devices(greet)

    def wait_all(buffer, count, sem):
        part = buffer.at[pl.ds(0, count)]
        pltpu.make_async_copy(part, part, sem).wait()

    loads[0].wait()
    lane = lax.broadcasted_iota(jnp.int32, (1, everyone), 1)
    own_row = jnp.zeros((1, everyone), jnp.int32)
    for j in range(stations):
        own_row = jnp.where(lane == stn * stations + j, ids_ref[j], own_row)
    id_rows[stn] = own_row

    loads[1].wait()
    wide_resp[...] = resp_in[...].astype(jnp.float32).reshape(stations * samples, width)

    def pack(wide, send, dst, pairs):
        for pair in pairs:
            first = dst * spd + 2 * pair
            both = jnp.concatenate(
                [wide[pl.ds(first + j, stations, stride=samples), :] for j in range(2)], axis=0
            )
            send[dst, pl.ds(2 * pair * stations, 2 * stations), :] = both.astype(jnp.bfloat16)

    def remote(src, dst_ref, group, device):
        pltpu.make_async_remote_copy(
            src_ref=src, dst_ref=dst_ref, send_sem=send_sem.at[group],
            recv_sem=recv_sem.at[group], device_id=device, device_id_type=MESH,
        ).start()

    pairs = spd // 2
    chunks = 2 if pairs % 2 == 0 else 1
    chunk_pairs = [range(c * pairs // chunks, (c + 1) * pairs // chunks) for c in range(chunks)]
    chunk_rows = [
        pl.ds(2 * part.start * stations, 2 * len(part) * stations) for part in chunk_pairs
    ]

    pl.semaphore_wait(barrier, devices - 1)

    def send_resp(dst):
        remote(id_rows.at[stn], id_rows.at[stn], IDS, {"stn": dst})
        pack(wide_resp, resp_send, dst, range(pairs))
        remote(resp_send.at[dst], resp_recv.at[stn], RESP, {"stn": dst})

    other_stations(send_resp)
    loads[2].wait()
    wide_volt[...] = volt_in[...].astype(jnp.float32).reshape(stations * samples, width)
    for chunk in range(chunks):

        def send_volt(dst, chunk=chunk):
            pack(wide_volt, volt_send, dst, chunk_pairs[chunk])
            part = chunk_rows[chunk]
            remote(volt_send.at[dst, part], volt_recv.at[stn, part], VOLT + chunk, {"stn": dst})

        other_stations(send_volt)
    pack(wide_resp, resp_send, stn, range(pairs))
    resp_recv[stn] = resp_send[stn]
    pack(wide_volt, volt_send, stn, range(pairs))
    volt_recv[stn] = volt_send[stn]

    loads[3].wait()
    flag = flags[...].astype(jnp.float32)
    mutual = (flag * flag.T).astype(jnp.bfloat16)
    wait_all(id_rows, n - 1, recv_sem.at[IDS])
    all_ids = jnp.sum(id_rows[...], axis=0)
    row = lax.broadcasted_iota(jnp.int32, (everyone, everyone), 0)
    column = lax.broadcasted_iota(jnp.int32, (everyone, everyone), 1)
    one_hot = (row == all_ids).astype(jnp.float32).astype(jnp.bfloat16)
    picked = dot(mutual, one_hot).T.astype(jnp.bfloat16)
    weight[...] = jnp.where(row == column, 0.0, dot(picked, one_hot))

    def unpack(recv, pair):
        block = recv[:, pl.ds(2 * pair * stations, 2 * stations), :].astype(jnp.float32)
        block = block.reshape(n, 2, stations, width)
        return [block[:, j].reshape(everyone, width) for j in range(2)]

    sign = jnp.where(lax.broadcasted_iota(jnp.int32, (1, width), 1) < half, -1.0, 1.0)
    loads[4].wait()
    loads[5].wait()
    steps = steps_ref[...].reshape(1, half)
    steps = jnp.concatenate([steps, steps], axis=1)

    def predict(t, gain_both, gain_turn):
        a = a_float[t]
        turned = gain_both * a + gain_turn * a_swap[t]
        applied[t, pl.ds(0, everyone), :] = turned.astype(jnp.bfloat16)
        applied[t, pl.ds(everyone, everyone), :] = (sign * pltpu.roll(turned, half, 1)).astype(jnp.bfloat16)
        return dot_last(applied[t, pl.ds(0, everyone), :], applied[t])

    def gain_parts(gain):
        swapped = pltpu.roll(gain, half, 1)
        left = sign < 0.0
        return jnp.where(left, gain, swapped), jnp.where(left, -swapped, gain)

    wait_all(resp_recv, n - 1, recv_sem.at[RESP])
    gain_both, gain_turn = gain_parts(gains[...])
    for pair in range(spd // 2):
        for j, a in enumerate(unpack(resp_recv, pair)):
            t = 2 * pair + j
            a_float[t] = a
            a_swap[t] = pltpu.roll(a, half, 1)
            diff[t] = predict(t, gain_both, gain_turn)

    def accumulate(t, totals):
        residual = jnp.concatenate(
            [
                (weight[...] * diff[t, :, pl.ds(0, everyone)]).astype(jnp.bfloat16),
                (weight[...] * diff[t, :, pl.ds(everyone, everyone)]).astype(jnp.bfloat16),
            ],
            axis=1,
        )
        hidden = dot(residual, applied[t])
        return totals[0] + a_float[t] * hidden, totals[1] + a_swap[t] * hidden

    def volt_chunk(chunk):
        part = volt_recv.at[pl.ds(0, n - 1), chunk_rows[chunk]]
        return pltpu.make_async_copy(part, part, recv_sem.at[VOLT + chunk])

    for iteration in range(ITERS):
        totals = (jnp.zeros((everyone, width), jnp.float32), jnp.zeros((everyone, width), jnp.float32))
        if iteration == 0:
            for chunk in range(chunks):
                volt_chunk(chunk).wait()
                for pair in chunk_pairs[chunk]:
                    for j, x in enumerate(unpack(volt_recv, pair)):
                        t = 2 * pair + j
                        mine = x.astype(jnp.bfloat16)
                        turned = (sign * pltpu.roll(x, half, 1)).astype(jnp.bfloat16)
                        seen = dot_last(mine, jnp.concatenate([mine, turned], axis=0))
                        observed[t] = seen
                        diff[t] = seen - diff[t]
                        totals = accumulate(t, totals)
        else:
            gain_both, gain_turn = gain_parts(current[...])
            for t in range(spd):
                diff[t] = observed[t] - predict(t, gain_both, gain_turn)
                totals = accumulate(t, totals)
        direct, crossed = totals
        energy = jnp.where(
            sign < 0.0,
            direct + pltpu.roll(direct, half, 1),
            crossed - pltpu.roll(crossed, half, 1),
        )
        energy_out[iteration] = energy.reshape(devices, rows, width)

        def send_sum(s, c):
            remote(
                energy_out.at[iteration, s * nchan + c], sums.at[iteration, me],
                SUMS + iteration, {"stn": s, "chan": c},
            )

        other_devices(send_sum)
        sums[iteration, me] = energy_out[iteration, me]
        wait_all(sums.at[iteration], devices - 1, recv_sem.at[SUMS + iteration])
        scale = -(2.0 / half) / half
        block = scale * jnp.sum(sums[iteration], axis=0)
        gathered[iteration, me] = block
        if iteration < ITERS - 1:

            def send_block(s, c):
                mine = gathered.at[iteration, me]
                remote(mine, mine, GATHER + iteration, {"stn": s, "chan": c})

            other_devices(send_block)
            wait_all(gathered.at[iteration], devices - 1, recv_sem.at[GATHER + iteration])
            gradient = gathered[iteration].reshape(everyone, width)
            spread = jnp.sqrt(jnp.sum(gradient * gradient, keepdims=True) / (everyone * half) + 1e-06)
            held = gains if iteration == 0 else current
            current[...] = held[...] - steps * (gradient / spread)
        else:
            norms[me] = jnp.sum(block * block, axis=0, keepdims=True)

            def send_norm(s, c):
                remote(norms.at[me], norms.at[me], NORM, {"stn": s, "chan": c})

            for c in range(1, nchan):
                mine = gathered.at[iteration, me]
                remote(mine, mine, GATHER + iteration, {"chan": lax.rem(chan + c, nchan)})
            other_devices(send_norm)
            wait_all(gathered.at[iteration], nchan - 1, recv_sem.at[GATHER + iteration])
            gradient = gathered[iteration, pl.ds(stn * nchan, nchan)].reshape(stations, width)
            own = current[pl.ds(pl.multiple_of(stn * stations, stations), stations), :]
            wait_all(norms, devices - 1, recv_sem.at[NORM])
            total = jnp.sum(jnp.sum(norms[...], axis=0), keepdims=True)
            spread = jnp.sqrt(total / (everyone * half) + 1e-06)
            descent = gradient / spread
            calibrated_ref[...] = own - steps * descent
            descent_ref[...] = descent

    wait_all(id_rows, n - 1, send_sem.at[IDS])
    wait_all(resp_send, n - 1, send_sem.at[RESP])
    for chunk in range(chunks):
        part = volt_send.at[pl.ds(0, n - 1), chunk_rows[chunk]]
        pltpu.make_async_copy(part, part, send_sem.at[VOLT + chunk]).wait()
    for iteration in range(ITERS):
        wait_all(sums.at[iteration], devices - 1, send_sem.at[SUMS + iteration])
        count = devices - 1 if iteration < ITERS - 1 else nchan - 1
        wait_all(gathered.at[iteration], count, send_sem.at[GATHER + iteration])
    wait_all(norms, devices - 1, send_sem.at[NORM])


def shards(n, nchan, voltages, response, start_gains, step_sizes, station_ids, baseline_flags):
    stations, width = voltages.shape[0], voltages.shape[3]
    samples = voltages.shape[1] * voltages.shape[2]
    everyone = stations * n
    devices = n * nchan
    spd = samples // n
    half = width // 2
    rows = stations // nchan
    f32, bf16 = jnp.float32, jnp.bfloat16
    hbm = pl.BlockSpec(memory_space=pltpu.HBM)
    vmem = pl.BlockSpec(memory_space=pltpu.VMEM)
    block = (n, spd * stations, width)
    scratch = [
        ((stations, samples, width), bf16),
        ((stations, samples, width), bf16),
        ((everyone, width), f32),
        ((everyone, everyone), jnp.int32),
        ((stations * samples, width), f32),
        ((stations * samples, width), f32),
        (block, bf16),
        (block, bf16),
        (block, bf16),
        (block, bf16),
        ((n, 1, everyone), jnp.int32),
        ((everyone, everyone), f32),
        ((spd, everyone, width), f32),
        ((spd, everyone, width), f32),
        ((spd, 2 * everyone, width), bf16),
        ((spd, everyone, 2 * everyone), f32),
        ((spd, everyone, 2 * everyone), f32),
        ((ITERS, devices, rows, width), f32),
        ((ITERS, devices, rows, width), f32),
        ((ITERS, devices, rows, width), f32),
        ((devices, 1, width), f32),
        ((everyone, width), f32),
        ((half,), f32),
    ]
    return pl.pallas_call(
        functools.partial(kernel, n, nchan, stations, samples),
        out_shape=[jax.ShapeDtypeStruct((stations, width), f32)] * 2,
        in_specs=[hbm] * 6,
        out_specs=[vmem, vmem],
        scratch_shapes=[pltpu.VMEM(shape, dtype) for shape, dtype in scratch]
        + [pltpu.SMEM((stations,), jnp.int32), pltpu.SemaphoreType.DMA((6,)), pltpu.SemaphoreType.DMA((GROUPS,)), pltpu.SemaphoreType.DMA((GROUPS,))],
        compiler_params=pltpu.CompilerParams(
            collective_id=0, has_side_effects=True, vmem_limit_bytes=48 * 1024 * 1024
        ),
    )(
        voltages.reshape(stations, samples, width),
        response.reshape(stations, samples, width),
        start_gains, step_sizes, station_ids, baseline_flags,
    )


def solution(mesh):
    placed = (P("stn", "chan", None, None), P("stn", "chan", None, None), P(), P(), P("stn"), P())
    return jax.shard_map(
        functools.partial(shards, mesh.shape["stn"], mesh.shape["chan"]),
        mesh=mesh,
        in_specs=placed,
        out_specs=(P("stn", None), P("stn", None)),
        check_vma=False,
    )
```

```python
import functools

import jax
import jax.numpy as jnp
from jax import lax
from jax.experimental import pallas as pl
from jax.experimental.pallas import tpu as pltpu
from jax.sharding import PartitionSpec as P

ITERS = 2
MESH = pl.DeviceIdType.MESH
IDS, RESP, VOLT, SUMS, GATHER = 0, 1, 2, 4, 4 + ITERS
NORM = GATHER + ITERS
GROUPS = NORM + 1


def dot_last(left, right):
    return lax.dot_general(left, right, (((1,), (1,)), ((), ())), preferred_element_type=jnp.float32)


def dot(left, right):
    return lax.dot_general(left, right, (((1,), (0,)), ((), ())), preferred_element_type=jnp.float32)


def kernel(
    n, nchan, stations, samples,
    volt_any, resp_any, gains_any, steps_any, ids_any, flags_any,
    calibrated_ref, descent_ref,
    volt_in, resp_in, gains, flags, wide_volt, wide_resp,
    volt_send, resp_send, volt_recv, resp_recv, id_rows,
    weight, a_float, a_swap, applied, observed, diff,
    energy_out, sums, gathered, norms, current, steps_ref, ids_ref,
    in_sem, send_sem, recv_sem,
):
    everyone = n * stations
    devices = n * nchan
    spd = samples // n
    rows = stations // nchan
    width = volt_in.shape[2]
    half = width // 2
    stn = lax.axis_index("stn")
    chan = lax.axis_index("chan")
    me = stn * nchan + chan

    def each(first, stop, body):
        if stop - first <= 16:
            quarter = max(stop // 4, 1)
            for k in sorted(range(first, stop), key=lambda k: (k % quarter, (2, 1, 3, 0).index(k // quarter % 4))):
                body(k)
        else:
            lax.fori_loop(first, stop, lambda k, carry: (body(k), carry)[1], 0)

    def other_stations(body):
        each(1, n, lambda k: body(lax.rem(stn + k, n)))

    def other_devices(body):
        each(1, n, lambda k: [body(lax.rem(stn + k, n), lax.rem(chan + c, nchan)) for c in range(nchan)])
        for c in range(1, nchan):
            body(stn, lax.rem(chan + c, nchan))

    loads = [
        pltpu.make_async_copy(src, dst, in_sem.at[i])
        for i, (src, dst) in enumerate(
            (
                (ids_any, ids_ref), (resp_any, resp_in), (volt_any, volt_in),
                (flags_any, flags), (gains_any, gains), (steps_any, steps_ref),
            )
        )
    ]
    for load in loads:
        load.start()

    barrier = pltpu.get_barrier_semaphore()

    def greet(s, c):
        pl.semaphore_signal(barrier, inc=1, device_id={"stn": s, "chan": c}, device_id_type=MESH)

    other_devices(greet)

    def wait_all(buffer, count, sem):
        part = buffer.at[pl.ds(0, count)]
        pltpu.make_async_copy(part, part, sem).wait()

    loads[0].wait()
    lane = lax.broadcasted_iota(jnp.int32, (1, everyone), 1)
    own_row = jnp.zeros((1, everyone), jnp.int32)
    for j in range(stations):
        own_row = jnp.where(lane == stn * stations + j, ids_ref[j], own_row)
    id_rows[stn] = own_row

    loads[1].wait()
    wide_resp[...] = resp_in[...].astype(jnp.float32).reshape(stations * samples, width)

    def pack(wide, send, dst, pairs):
        for pair in pairs:
            first = dst * spd + 2 * pair
            both = jnp.concatenate(
                [wide[pl.ds(first + j, stations, stride=samples), :] for j in range(2)], axis=0
            )
            send[dst, pl.ds(2 * pair * stations, 2 * stations), :] = both.astype(jnp.bfloat16)

    def remote(src, dst_ref, group, device):
        pltpu.make_async_remote_copy(
            src_ref=src, dst_ref=dst_ref, send_sem=send_sem.at[group],
            recv_sem=recv_sem.at[group], device_id=device, device_id_type=MESH,
        ).start()

    pairs = spd // 2
    chunks = 2 if pairs % 2 == 0 else 1
    chunk_pairs = [range(c * pairs // chunks, (c + 1) * pairs // chunks) for c in range(chunks)]
    chunk_rows = [
        pl.ds(2 * part.start * stations, 2 * len(part) * stations) for part in chunk_pairs
    ]

    pl.semaphore_wait(barrier, devices - 1)

    def send_resp(dst):
        remote(id_rows.at[stn], id_rows.at[stn], IDS, {"stn": dst})
        pack(wide_resp, resp_send, dst, range(pairs))
        remote(resp_send.at[dst], resp_recv.at[stn], RESP, {"stn": dst})

    other_stations(send_resp)
    loads[2].wait()
    wide_volt[...] = volt_in[...].astype(jnp.float32).reshape(stations * samples, width)
    for chunk in range(chunks):

        def send_volt(dst, chunk=chunk):
            pack(wide_volt, volt_send, dst, chunk_pairs[chunk])
            part = chunk_rows[chunk]
            remote(volt_send.at[dst, part], volt_recv.at[stn, part], VOLT + chunk, {"stn": dst})

        other_stations(send_volt)
    pack(wide_resp, resp_send, stn, range(pairs))
    resp_recv[stn] = resp_send[stn]
    pack(wide_volt, volt_send, stn, range(pairs))
    volt_recv[stn] = volt_send[stn]

    loads[3].wait()
    flag = flags[...].astype(jnp.float32)
    mutual = (flag * flag.T).astype(jnp.bfloat16)
    wait_all(id_rows, n - 1, recv_sem.at[IDS])
    all_ids = jnp.sum(id_rows[...], axis=0)
    row = lax.broadcasted_iota(jnp.int32, (everyone, everyone), 0)
    column = lax.broadcasted_iota(jnp.int32, (everyone, everyone), 1)
    one_hot = (row == all_ids).astype(jnp.float32).astype(jnp.bfloat16)
    picked = dot(mutual, one_hot).T.astype(jnp.bfloat16)
    weight[...] = jnp.where(row == column, 0.0, dot(picked, one_hot))

    def unpack(recv, pair):
        block = recv[:, pl.ds(2 * pair * stations, 2 * stations), :].astype(jnp.float32)
        block = block.reshape(n, 2, stations, width)
        return [block[:, j].reshape(everyone, width) for j in range(2)]

    sign = jnp.where(lax.broadcasted_iota(jnp.int32, (1, width), 1) < half, -1.0, 1.0)
    loads[4].wait()
    loads[5].wait()
    steps = steps_ref[...].reshape(1, half)
    steps = jnp.concatenate([steps, steps], axis=1)

    def predict(t, gain_both, gain_turn):
        a = a_float[t]
        turned = gain_both * a + gain_turn * a_swap[t]
        applied[t, pl.ds(0, everyone), :] = turned.astype(jnp.bfloat16)
        applied[t, pl.ds(everyone, everyone), :] = (sign * pltpu.roll(turned, half, 1)).astype(jnp.bfloat16)
        return dot_last(applied[t, pl.ds(0, everyone), :], applied[t])

    def gain_parts(gain):
        swapped = pltpu.roll(gain, half, 1)
        left = sign < 0.0
        return jnp.where(left, gain, swapped), jnp.where(left, -swapped, gain)

    wait_all(resp_recv, n - 1, recv_sem.at[RESP])
    gain_both, gain_turn = gain_parts(gains[...])
    for pair in range(spd // 2):
        for j, a in enumerate(unpack(resp_recv, pair)):
            t = 2 * pair + j
            a_float[t] = a
            a_swap[t] = pltpu.roll(a, half, 1)
            diff[t] = predict(t, gain_both, gain_turn)

    def accumulate(t, totals):
        residual = jnp.concatenate(
            [
                (weight[...] * diff[t, :, pl.ds(0, everyone)]).astype(jnp.bfloat16),
                (weight[...] * diff[t, :, pl.ds(everyone, everyone)]).astype(jnp.bfloat16),
            ],
            axis=1,
        )
        hidden = dot(residual, applied[t])
        return totals[0] + a_float[t] * hidden, totals[1] + a_swap[t] * hidden

    def volt_chunk(chunk):
        part = volt_recv.at[pl.ds(0, n - 1), chunk_rows[chunk]]
        return pltpu.make_async_copy(part, part, recv_sem.at[VOLT + chunk])

    for iteration in range(ITERS):
        totals = (jnp.zeros((everyone, width), jnp.float32), jnp.zeros((everyone, width), jnp.float32))
        if iteration == 0:
            for chunk in range(chunks):
                volt_chunk(chunk).wait()
                for pair in chunk_pairs[chunk]:
                    for j, x in enumerate(unpack(volt_recv, pair)):
                        t = 2 * pair + j
                        mine = x.astype(jnp.bfloat16)
                        turned = (sign * pltpu.roll(x, half, 1)).astype(jnp.bfloat16)
                        seen = dot_last(mine, jnp.concatenate([mine, turned], axis=0))
                        observed[t] = seen
                        diff[t] = seen - diff[t]
                        totals = accumulate(t, totals)
        else:
            gain_both, gain_turn = gain_parts(current[...])
            for t in range(spd):
                diff[t] = observed[t] - predict(t, gain_both, gain_turn)
                totals = accumulate(t, totals)
        direct, crossed = totals
        energy = jnp.where(
            sign < 0.0,
            direct + pltpu.roll(direct, half, 1),
            crossed - pltpu.roll(crossed, half, 1),
        )
        energy_out[iteration] = energy.reshape(devices, rows, width)

        def send_sum(s, c):
            remote(
                energy_out.at[iteration, s * nchan + c], sums.at[iteration, me],
                SUMS + iteration, {"stn": s, "chan": c},
            )

        other_devices(send_sum)
        sums[iteration, me] = energy_out[iteration, me]
        wait_all(sums.at[iteration], devices - 1, recv_sem.at[SUMS + iteration])
        scale = -(2.0 / half) / half
        block = scale * jnp.sum(sums[iteration], axis=0)
        gathered[iteration, me] = block
        if iteration < ITERS - 1:

            def send_block(s, c):
                mine = gathered.at[iteration, me]
                remote(mine, mine, GATHER + iteration, {"stn": s, "chan": c})

            other_devices(send_block)
            wait_all(gathered.at[iteration], devices - 1, recv_sem.at[GATHER + iteration])
            gradient = gathered[iteration].reshape(everyone, width)
            spread = jnp.sqrt(jnp.sum(gradient * gradient, keepdims=True) / (everyone * half) + 1e-06)
            held = gains if iteration == 0 else current
            current[...] = held[...] - steps * (gradient / spread)
        else:
            norms[me] = jnp.sum(block * block, axis=0, keepdims=True)

            def send_norm(s, c):
                remote(norms.at[me], norms.at[me], NORM, {"stn": s, "chan": c})

            for c in range(1, nchan):
                mine = gathered.at[iteration, me]
                remote(mine, mine, GATHER + iteration, {"chan": lax.rem(chan + c, nchan)})
            other_devices(send_norm)
            wait_all(gathered.at[iteration], nchan - 1, recv_sem.at[GATHER + iteration])
            gradient = gathered[iteration, pl.ds(stn * nchan, nchan)].reshape(stations, width)
            own = current[pl.ds(pl.multiple_of(stn * stations, stations), stations), :]
            wait_all(norms, devices - 1, recv_sem.at[NORM])
            total = jnp.sum(jnp.sum(norms[...], axis=0), keepdims=True)
            spread = jnp.sqrt(total / (everyone * half) + 1e-06)
            descent = gradient / spread
            calibrated_ref[...] = own - steps * descent
            descent_ref[...] = descent

    wait_all(id_rows, n - 1, send_sem.at[IDS])
    wait_all(resp_send, n - 1, send_sem.at[RESP])
    for chunk in range(chunks):
        part = volt_send.at[pl.ds(0, n - 1), chunk_rows[chunk]]
        pltpu.make_async_copy(part, part, send_sem.at[VOLT + chunk]).wait()
    for iteration in range(ITERS):
        wait_all(sums.at[iteration], devices - 1, send_sem.at[SUMS + iteration])
        count = devices - 1 if iteration < ITERS - 1 else nchan - 1
        wait_all(gathered.at[iteration], count, send_sem.at[GATHER + iteration])
    wait_all(norms, devices - 1, send_sem.at[NORM])


def shards(n, nchan, voltages, response, start_gains, step_sizes, station_ids, baseline_flags):
    stations, width = voltages.shape[0], voltages.shape[3]
    samples = voltages.shape[1] * voltages.shape[2]
    everyone = stations * n
    devices = n * nchan
    spd = samples // n
    half = width // 2
    rows = stations // nchan
    f32, bf16 = jnp.float32, jnp.bfloat16
    hbm = pl.BlockSpec(memory_space=pltpu.HBM)
    vmem = pl.BlockSpec(memory_space=pltpu.VMEM)
    block = (n, spd * stations, width)
    scratch = [
        ((stations, samples, width), bf16),
        ((stations, samples, width), bf16),
        ((everyone, width), f32),
        ((everyone, everyone), jnp.int32),
        ((stations * samples, width), f32),
        ((stations * samples, width), f32),
        (block, bf16),
        (block, bf16),
        (block, bf16),
        (block, bf16),
        ((n, 1, everyone), jnp.int32),
        ((everyone, everyone), f32),
        ((spd, everyone, width), f32),
        ((spd, everyone, width), f32),
        ((spd, 2 * everyone, width), bf16),
        ((spd, everyone, 2 * everyone), f32),
        ((spd, everyone, 2 * everyone), f32),
        ((ITERS, devices, rows, width), f32),
        ((ITERS, devices, rows, width), f32),
        ((ITERS, devices, rows, width), f32),
        ((devices, 1, width), f32),
        ((everyone, width), f32),
        ((half,), f32),
    ]
    return pl.pallas_call(
        functools.partial(kernel, n, nchan, stations, samples),
        out_shape=[jax.ShapeDtypeStruct((stations, width), f32)] * 2,
        in_specs=[hbm] * 6,
        out_specs=[vmem, vmem],
        scratch_shapes=[pltpu.VMEM(shape, dtype) for shape, dtype in scratch]
        + [pltpu.SMEM((stations,), jnp.int32), pltpu.SemaphoreType.DMA((6,)), pltpu.SemaphoreType.DMA((GROUPS,)), pltpu.SemaphoreType.DMA((GROUPS,))],
        compiler_params=pltpu.CompilerParams(
            collective_id=0, has_side_effects=True, vmem_limit_bytes=64 * 1024 * 1024
        ),
    )(
        voltages.reshape(stations, samples, width),
        response.reshape(stations, samples, width),
        start_gains, step_sizes, station_ids, baseline_flags,
    )


def solution(mesh):
    placed = (P("stn", "chan", None, None), P("stn", "chan", None, None), P(), P(), P("stn"), P())
    return jax.shard_map(
        functools.partial(shards, mesh.shape["stn"], mesh.shape["chan"]),
        mesh=mesh,
        in_specs=placed,
        out_specs=(P("stn", None), P("stn", None)),
        check_vma=False,
    )
```

```python
import functools

import jax
import jax.numpy as jnp
from jax import lax
from jax.experimental import pallas as pl
from jax.experimental.pallas import tpu as pltpu
from jax.sharding import PartitionSpec as P

ITERS = 2
MESH = pl.DeviceIdType.MESH
IDS, RESP, VOLT, PAIR = 0, 1, 2, 4
SUMS = PAIR + ITERS
GATHER = SUMS + ITERS
GROUPS = GATHER + ITERS


def dot_last(left, right):
    return lax.dot_general(left, right, (((1,), (1,)), ((), ())), preferred_element_type=jnp.float32)


def dot(left, right):
    return lax.dot_general(left, right, (((1,), (0,)), ((), ())), preferred_element_type=jnp.float32)


def kernel(
    n, nchan, stations, samples,
    volt_any, resp_any, gains_any, steps_any, ids_any, flags_any,
    calibrated_ref, descent_ref,
    volt_in, resp_in, gains, flags, wide_volt, wide_resp,
    volt_send, resp_send, volt_recv, resp_recv, id_rows,
    weight, a_float, a_swap, applied, observed, diff,
    energies, chip_sum, sums, gathered, norms, current, steps_ref, ids_ref,
    in_sem, send_sem, recv_sem,
):
    everyone = n * stations
    spd = samples // n
    width = volt_in.shape[2]
    half = width // 2
    stn = lax.axis_index("stn")
    chan = lax.axis_index("chan")

    def each(first, stop, body):
        if stop - first <= 16:
            quarter = max(stop // 4, 1)
            for k in sorted(range(first, stop), key=lambda k: (k % quarter, (2, 1, 3, 0).index(k // quarter % 4))):
                body(k)
        else:
            lax.fori_loop(first, stop, lambda k, carry: (body(k), carry)[1], 0)

    def other_stations(body):
        each(1, n, lambda k: body(lax.rem(stn + k, n)))

    def other_chans(body):
        for c in range(1, nchan):
            body(lax.rem(chan + c, nchan))

    loads = [
        pltpu.make_async_copy(src, dst, in_sem.at[i])
        for i, (src, dst) in enumerate(
            (
                (ids_any, ids_ref), (resp_any, resp_in), (volt_any, volt_in),
                (flags_any, flags), (gains_any, gains), (steps_any, steps_ref),
            )
        )
    ]
    for load in loads:
        load.start()

    barrier = pltpu.get_barrier_semaphore()

    def greet(device):
        pl.semaphore_signal(barrier, inc=1, device_id=device, device_id_type=MESH)

    other_stations(lambda s: greet({"stn": s}))
    other_chans(lambda c: greet({"chan": c}))

    def wait_all(buffer, count, sem):
        part = buffer.at[pl.ds(0, count)]
        pltpu.make_async_copy(part, part, sem).wait()

    loads[0].wait()
    lane = lax.broadcasted_iota(jnp.int32, (1, everyone), 1)
    own_row = jnp.zeros((1, everyone), jnp.int32)
    for j in range(stations):
        own_row = jnp.where(lane == stn * stations + j, ids_ref[j], own_row)
    id_rows[stn] = own_row

    loads[1].wait()
    wide_resp[...] = resp_in[...].astype(jnp.float32).reshape(stations * samples, width)

    def pack(wide, send, dst, pairs):
        for pair in pairs:
            first = dst * spd + 2 * pair
            both = jnp.concatenate(
                [wide[pl.ds(first + j, stations, stride=samples), :] for j in range(2)], axis=0
            )
            send[dst, pl.ds(2 * pair * stations, 2 * stations), :] = both.astype(jnp.bfloat16)

    def remote(src, dst_ref, group, device):
        pltpu.make_async_remote_copy(
            src_ref=src, dst_ref=dst_ref, send_sem=send_sem.at[group],
            recv_sem=recv_sem.at[group], device_id=device, device_id_type=MESH,
        ).start()

    pairs = spd // 2
    chunks = 2 if pairs % 2 == 0 else 1
    chunk_pairs = [range(c * pairs // chunks, (c + 1) * pairs // chunks) for c in range(chunks)]
    chunk_rows = [
        pl.ds(2 * part.start * stations, 2 * len(part) * stations) for part in chunk_pairs
    ]

    pl.semaphore_wait(barrier, n + nchan - 2)

    def send_resp(dst):
        remote(id_rows.at[stn], id_rows.at[stn], IDS, {"stn": dst})
        pack(wide_resp, resp_send, dst, range(pairs))
        remote(resp_send.at[dst], resp_recv.at[stn], RESP, {"stn": dst})

    other_stations(send_resp)
    loads[2].wait()
    wide_volt[...] = volt_in[...].astype(jnp.float32).reshape(stations * samples, width)
    for chunk in range(chunks):

        def send_volt(dst, chunk=chunk):
            pack(wide_volt, volt_send, dst, chunk_pairs[chunk])
            part = chunk_rows[chunk]
            remote(volt_send.at[dst, part], volt_recv.at[stn, part], VOLT + chunk, {"stn": dst})

        other_stations(send_volt)
    pack(wide_resp, resp_send, stn, range(pairs))
    resp_recv[stn] = resp_send[stn]
    pack(wide_volt, volt_send, stn, range(pairs))
    volt_recv[stn] = volt_send[stn]

    loads[3].wait()
    flag = flags[...].astype(jnp.float32)
    mutual = (flag * flag.T).astype(jnp.bfloat16)
    wait_all(id_rows, n - 1, recv_sem.at[IDS])
    all_ids = jnp.sum(id_rows[...], axis=0)
    row = lax.broadcasted_iota(jnp.int32, (everyone, everyone), 0)
    column = lax.broadcasted_iota(jnp.int32, (everyone, everyone), 1)
    one_hot = (row == all_ids).astype(jnp.float32).astype(jnp.bfloat16)
    picked = dot(mutual, one_hot).T.astype(jnp.bfloat16)
    weight[...] = jnp.where(row == column, 0.0, dot(picked, one_hot))

    def unpack(recv, pair):
        block = recv[:, pl.ds(2 * pair * stations, 2 * stations), :].astype(jnp.float32)
        block = block.reshape(n, 2, stations, width)
        return [block[:, j].reshape(everyone, width) for j in range(2)]

    sign = jnp.where(lax.broadcasted_iota(jnp.int32, (1, width), 1) < half, -1.0, 1.0)
    loads[4].wait()
    loads[5].wait()
    steps = steps_ref[...].reshape(1, half)
    steps = jnp.concatenate([steps, steps], axis=1)

    def predict(t, gain_both, gain_turn):
        a = a_float[t]
        turned = gain_both * a + gain_turn * a_swap[t]
        applied[t, pl.ds(0, everyone), :] = turned.astype(jnp.bfloat16)
        applied[t, pl.ds(everyone, everyone), :] = (sign * pltpu.roll(turned, half, 1)).astype(jnp.bfloat16)
        return dot_last(applied[t, pl.ds(0, everyone), :], applied[t])

    def gain_parts(gain):
        swapped = pltpu.roll(gain, half, 1)
        left = sign < 0.0
        return jnp.where(left, gain, swapped), jnp.where(left, -swapped, gain)

    wait_all(resp_recv, n - 1, recv_sem.at[RESP])
    gain_both, gain_turn = gain_parts(gains[...])
    for pair in range(spd // 2):
        for j, a in enumerate(unpack(resp_recv, pair)):
            t = 2 * pair + j
            a_float[t] = a
            a_swap[t] = pltpu.roll(a, half, 1)
            diff[t] = predict(t, gain_both, gain_turn)

    def accumulate(t, totals):
        residual = jnp.concatenate(
            [
                (weight[...] * diff[t, :, pl.ds(0, everyone)]).astype(jnp.bfloat16),
                (weight[...] * diff[t, :, pl.ds(everyone, everyone)]).astype(jnp.bfloat16),
            ],
            axis=1,
        )
        hidden = dot(residual, applied[t])
        return totals[0] + a_float[t] * hidden, totals[1] + a_swap[t] * hidden

    def volt_chunk(chunk):
        part = volt_recv.at[pl.ds(0, n - 1), chunk_rows[chunk]]
        return pltpu.make_async_copy(part, part, recv_sem.at[VOLT + chunk])

    for iteration in range(ITERS):
        totals = (jnp.zeros((everyone, width), jnp.float32), jnp.zeros((everyone, width), jnp.float32))
        if iteration == 0:
            for chunk in range(chunks):
                volt_chunk(chunk).wait()
                for pair in chunk_pairs[chunk]:
                    for j, x in enumerate(unpack(volt_recv, pair)):
                        t = 2 * pair + j
                        mine = x.astype(jnp.bfloat16)
                        turned = (sign * pltpu.roll(x, half, 1)).astype(jnp.bfloat16)
                        seen = dot_last(mine, jnp.concatenate([mine, turned], axis=0))
                        observed[t] = seen
                        diff[t] = seen - diff[t]
                        totals = accumulate(t, totals)
        else:
            gain_both, gain_turn = gain_parts(current[...])
            for t in range(spd):
                diff[t] = observed[t] - predict(t, gain_both, gain_turn)
                totals = accumulate(t, totals)
        direct, crossed = totals
        energy = jnp.where(
            sign < 0.0,
            direct + pltpu.roll(direct, half, 1),
            crossed - pltpu.roll(crossed, half, 1),
        )
        energies[iteration, chan] = energy.reshape(n, stations, width)
        mine = energies.at[iteration, chan]
        other_chans(lambda c: remote(mine, mine, PAIR + iteration, {"chan": c}))
        wait_all(energies.at[iteration], nchan - 1, recv_sem.at[PAIR + iteration])
        chip_sum[iteration] = jnp.sum(energies[iteration], axis=0)
        other_stations(
            lambda s: remote(
                chip_sum.at[iteration, s], sums.at[iteration, stn], SUMS + iteration, {"stn": s}
            )
        )
        sums[iteration, stn] = chip_sum[iteration, stn]
        wait_all(sums.at[iteration], n - 1, recv_sem.at[SUMS + iteration])
        scale = -(2.0 / half) / half
        block = scale * jnp.sum(sums[iteration], axis=0)
        if iteration < ITERS - 1:
            gathered[iteration, stn] = block
            part = gathered.at[iteration, stn]
            other_stations(lambda s: remote(part, part, GATHER + iteration, {"stn": s}))
            wait_all(gathered.at[iteration], n - 1, recv_sem.at[GATHER + iteration])
            gradient = gathered[iteration].reshape(everyone, width)
            spread = jnp.sqrt(jnp.sum(gradient * gradient, keepdims=True) / (everyone * half) + 1e-06)
            held = gains if iteration == 0 else current
            current[...] = held[...] - steps * (gradient / spread)
        else:
            norms[stn] = jnp.sum(block * block, axis=0, keepdims=True)
            part = norms.at[stn]
            other_stations(lambda s: remote(part, part, GATHER + iteration, {"stn": s}))
            own = current[pl.ds(pl.multiple_of(stn * stations, stations), stations), :]
            wait_all(norms, n - 1, recv_sem.at[GATHER + iteration])
            total = jnp.sum(jnp.sum(norms[...], axis=0), keepdims=True)
            spread = jnp.sqrt(total / (everyone * half) + 1e-06)
            descent = block / spread
            calibrated_ref[...] = own - steps * descent
            descent_ref[...] = descent

    wait_all(id_rows, n - 1, send_sem.at[IDS])
    wait_all(resp_send, n - 1, send_sem.at[RESP])
    for chunk in range(chunks):
        part = volt_send.at[pl.ds(0, n - 1), chunk_rows[chunk]]
        pltpu.make_async_copy(part, part, send_sem.at[VOLT + chunk]).wait()
    for iteration in range(ITERS):
        wait_all(energies.at[iteration], nchan - 1, send_sem.at[PAIR + iteration])
        wait_all(sums.at[iteration], n - 1, send_sem.at[SUMS + iteration])
        last = gathered.at[iteration] if iteration < ITERS - 1 else norms
        wait_all(last, n - 1, send_sem.at[GATHER + iteration])


def shards(n, nchan, voltages, response, start_gains, step_sizes, station_ids, baseline_flags):
    stations, width = voltages.shape[0], voltages.shape[3]
    samples = voltages.shape[1] * voltages.shape[2]
    everyone = stations * n
    spd = samples // n
    half = width // 2
    f32, bf16 = jnp.float32, jnp.bfloat16
    hbm = pl.BlockSpec(memory_space=pltpu.HBM)
    vmem = pl.BlockSpec(memory_space=pltpu.VMEM)
    block = (n, spd * stations, width)
    scratch = [
        ((stations, samples, width), bf16),
        ((stations, samples, width), bf16),
        ((everyone, width), f32),
        ((everyone, everyone), jnp.int32),
        ((stations * samples, width), f32),
        ((stations * samples, width), f32),
        (block, bf16),
        (block, bf16),
        (block, bf16),
        (block, bf16),
        ((n, 1, everyone), jnp.int32),
        ((everyone, everyone), f32),
        ((spd, everyone, width), f32),
        ((spd, everyone, width), f32),
        ((spd, 2 * everyone, width), bf16),
        ((spd, everyone, 2 * everyone), f32),
        ((spd, everyone, 2 * everyone), f32),
        ((ITERS, nchan, n, stations, width), f32),
        ((ITERS, n, stations, width), f32),
        ((ITERS, n, stations, width), f32),
        ((ITERS - 1, n, stations, width), f32),
        ((n, 1, width), f32),
        ((everyone, width), f32),
        ((half,), f32),
    ]
    return pl.pallas_call(
        functools.partial(kernel, n, nchan, stations, samples),
        out_shape=[jax.ShapeDtypeStruct((stations, width), f32)] * 2,
        in_specs=[hbm] * 6,
        out_specs=[vmem, vmem],
        scratch_shapes=[pltpu.VMEM(shape, dtype) for shape, dtype in scratch]
        + [pltpu.SMEM((stations,), jnp.int32), pltpu.SemaphoreType.DMA((6,)), pltpu.SemaphoreType.DMA((GROUPS,)), pltpu.SemaphoreType.DMA((GROUPS,))],
        compiler_params=pltpu.CompilerParams(
            collective_id=0, has_side_effects=True, vmem_limit_bytes=64 * 1024 * 1024
        ),
    )(
        voltages.reshape(stations, samples, width),
        response.reshape(stations, samples, width),
        start_gains, step_sizes, station_ids, baseline_flags,
    )


def solution(mesh):
    placed = (P("stn", "chan", None, None), P("stn", "chan", None, None), P(), P(), P("stn"), P())
    return jax.shard_map(
        functools.partial(shards, mesh.shape["stn"], mesh.shape["chan"]),
        mesh=mesh,
        in_specs=placed,
        out_specs=(P("stn", None), P("stn", None)),
        check_vma=False,
    )
```

```python
import functools

import jax
import jax.numpy as jnp
from jax import lax
from jax.experimental import pallas as pl
from jax.experimental.pallas import tpu as pltpu
from jax.sharding import PartitionSpec as P

ITERS = 2
MESH = pl.DeviceIdType.MESH
IDS, RESP, VOLT, PAIR = 0, 1, 2, 4
SUMS = PAIR + ITERS
GATHER = SUMS + ITERS
GROUPS = GATHER + ITERS


def dot_last(left, right):
    return lax.dot_general(left, right, (((1,), (1,)), ((), ())), preferred_element_type=jnp.float32)


def dot(left, right):
    return lax.dot_general(left, right, (((1,), (0,)), ((), ())), preferred_element_type=jnp.float32)


def kernel(
    n, nchan, stations, samples,
    volt_any, resp_any, gains_any, steps_any, ids_any, flags_any,
    result_ref,
    volt_in, resp_in, gains, flags, wide_volt, wide_resp,
    volt_send, resp_send, volt_recv, resp_recv, id_rows,
    weight, a_float, a_swap, applied, observed, diff,
    energies, chip_sum, sums, gathered, norms, current, steps_ref, ids_ref,
    in_sem, send_sem, recv_sem,
):
    everyone = n * stations
    spd = samples // n
    width = volt_in.shape[2]
    half = width // 2
    stn = lax.axis_index("stn")
    chan = lax.axis_index("chan")

    def each(first, stop, body):
        lax.fori_loop(first, stop, lambda k, carry: (body(k), carry)[1], 0)

    def other_stations(body):
        quarter = n // 4
        each(0, quarter, lambda k: [body(lax.rem(stn + far * quarter + k, n)) for far in (2, 1, 3)])
        each(1, quarter, lambda k: body(lax.rem(stn + k, n)))

    def other_chans(body):
        for c in range(1, nchan):
            body(lax.rem(chan + c, nchan))

    loads = [
        pltpu.make_async_copy(src, dst, in_sem.at[i])
        for i, (src, dst) in enumerate(
            (
                (ids_any, ids_ref), (resp_any, resp_in), (volt_any, volt_in),
                (flags_any, flags), (gains_any, gains), (steps_any, steps_ref),
            )
        )
    ]
    for load in loads:
        load.start()

    barrier = pltpu.get_barrier_semaphore()

    def greet(device):
        pl.semaphore_signal(barrier, inc=1, device_id=device, device_id_type=MESH)

    other_stations(lambda s: greet({"stn": s}))
    other_chans(lambda c: greet({"chan": c}))

    def wait_all(buffer, count, sem):
        part = buffer.at[pl.ds(0, count)]
        pltpu.make_async_copy(part, part, sem).wait()

    loads[0].wait()
    lane = lax.broadcasted_iota(jnp.int32, (1, everyone), 1)
    own_row = jnp.zeros((1, everyone), jnp.int32)
    for j in range(stations):
        own_row = jnp.where(lane == stn * stations + j, ids_ref[j], own_row)
    id_rows[stn] = own_row

    loads[1].wait()
    wide_resp[...] = resp_in[...].astype(jnp.float32).reshape(stations * samples, width)

    def pack(wide, send, dst, pairs):
        for pair in pairs:
            first = dst * spd + 2 * pair
            both = jnp.concatenate(
                [wide[pl.ds(first + j, stations, stride=samples), :] for j in range(2)], axis=0
            )
            send[dst, pl.ds(2 * pair * stations, 2 * stations), :] = both.astype(jnp.bfloat16)

    def remote(src, dst_ref, group, device):
        pltpu.make_async_remote_copy(
            src_ref=src, dst_ref=dst_ref, send_sem=send_sem.at[group],
            recv_sem=recv_sem.at[group], device_id=device, device_id_type=MESH,
        ).start()

    pairs = spd // 2
    chunks = 2 if pairs % 2 == 0 else 1
    chunk_pairs = [range(c * pairs // chunks, (c + 1) * pairs // chunks) for c in range(chunks)]
    chunk_rows = [
        pl.ds(2 * part.start * stations, 2 * len(part) * stations) for part in chunk_pairs
    ]

    pl.semaphore_wait(barrier, n + nchan - 2)

    def send_resp(dst):
        remote(id_rows.at[stn], id_rows.at[stn], IDS, {"stn": dst})
        pack(wide_resp, resp_send, dst, range(pairs))
        remote(resp_send.at[dst], resp_recv.at[stn], RESP, {"stn": dst})

    other_stations(send_resp)
    loads[2].wait()
    wide_volt[...] = volt_in[...].astype(jnp.float32).reshape(stations * samples, width)
    for chunk in range(chunks):

        def send_volt(dst, chunk=chunk):
            pack(wide_volt, volt_send, dst, chunk_pairs[chunk])
            part = chunk_rows[chunk]
            remote(volt_send.at[dst, part], volt_recv.at[stn, part], VOLT + chunk, {"stn": dst})

        other_stations(send_volt)
    pack(wide_resp, resp_send, stn, range(pairs))
    resp_recv[stn] = resp_send[stn]
    pack(wide_volt, volt_send, stn, range(pairs))
    volt_recv[stn] = volt_send[stn]

    loads[3].wait()
    flag = flags[...].astype(jnp.float32)
    mutual = (flag * flag.T).astype(jnp.bfloat16)
    wait_all(id_rows, n - 1, recv_sem.at[IDS])
    all_ids = jnp.sum(id_rows[...], axis=0)
    row = lax.broadcasted_iota(jnp.int32, (everyone, everyone), 0)
    column = lax.broadcasted_iota(jnp.int32, (everyone, everyone), 1)
    one_hot = (row == all_ids).astype(jnp.float32).astype(jnp.bfloat16)
    picked = dot(mutual, one_hot).T.astype(jnp.bfloat16)
    weight[...] = jnp.where(row == column, 0.0, dot(picked, one_hot))

    def unpack(recv, pair):
        at = pl.ds(pl.multiple_of(2 * pair * stations, 2 * stations), 2 * stations)
        block = recv[:, at, :].astype(jnp.float32)
        block = block.reshape(n, 2, stations, width)
        return [block[:, j].reshape(everyone, width) for j in range(2)]

    sign = jnp.where(lax.broadcasted_iota(jnp.int32, (1, width), 1) < half, -1.0, 1.0)
    loads[4].wait()
    loads[5].wait()
    steps = steps_ref[...].reshape(1, half)
    steps = jnp.concatenate([steps, steps], axis=1)

    def predict(t, gain_both, gain_turn):
        a = a_float[t]
        turned = gain_both * a + gain_turn * a_swap[t]
        applied[t, pl.ds(0, everyone), :] = turned.astype(jnp.bfloat16)
        applied[t, pl.ds(everyone, everyone), :] = (sign * pltpu.roll(turned, half, 1)).astype(jnp.bfloat16)
        return dot_last(applied[t, pl.ds(0, everyone), :], applied[t])

    def gain_parts(gain):
        swapped = pltpu.roll(gain, half, 1)
        left = sign < 0.0
        return jnp.where(left, gain, swapped), jnp.where(left, -swapped, gain)

    wait_all(resp_recv, n - 1, recv_sem.at[RESP])
    gain_both, gain_turn = gain_parts(gains[...])

    def first_predictions(pair):
        for j, a in enumerate(unpack(resp_recv, pair)):
            t = 2 * pair + j
            a_float[t] = a
            a_swap[t] = pltpu.roll(a, half, 1)
            diff[t] = predict(t, gain_both, gain_turn)

    each(0, pairs, first_predictions)

    def accumulate(t, totals):
        residual = jnp.concatenate(
            [
                (weight[...] * diff[t, :, pl.ds(0, everyone)]).astype(jnp.bfloat16),
                (weight[...] * diff[t, :, pl.ds(everyone, everyone)]).astype(jnp.bfloat16),
            ],
            axis=1,
        )
        hidden = dot(residual, applied[t])
        return totals[0] + a_float[t] * hidden, totals[1] + a_swap[t] * hidden

    def observe(pair, totals):
        for j, x in enumerate(unpack(volt_recv, pair)):
            t = 2 * pair + j
            mine = x.astype(jnp.bfloat16)
            turned = (sign * pltpu.roll(x, half, 1)).astype(jnp.bfloat16)
            seen = dot_last(mine, jnp.concatenate([mine, turned], axis=0))
            observed[t] = seen
            diff[t] = seen - diff[t]
        for t in (2 * pair, 2 * pair + 1):
            totals = accumulate(t, totals)
        return totals

    def volt_chunk(chunk):
        part = volt_recv.at[pl.ds(0, n - 1), chunk_rows[chunk]]
        return pltpu.make_async_copy(part, part, recv_sem.at[VOLT + chunk])

    for iteration in range(ITERS):
        totals = (jnp.zeros((everyone, width), jnp.float32), jnp.zeros((everyone, width), jnp.float32))
        if iteration == 0:
            for chunk in range(chunks):
                volt_chunk(chunk).wait()
                part = chunk_pairs[chunk]
                totals = lax.fori_loop(part.start, part.stop, observe, totals)
        else:
            gain_both, gain_turn = gain_parts(current[...])

            def again(pair, totals, gain_both=gain_both, gain_turn=gain_turn):
                for t in (2 * pair, 2 * pair + 1):
                    diff[t] = observed[t] - predict(t, gain_both, gain_turn)
                for t in (2 * pair, 2 * pair + 1):
                    totals = accumulate(t, totals)
                return totals

            totals = lax.fori_loop(0, pairs, again, totals)
        direct, crossed = totals
        energy = jnp.where(
            sign < 0.0,
            direct + pltpu.roll(direct, half, 1),
            crossed - pltpu.roll(crossed, half, 1),
        )
        energies[iteration, chan] = energy.reshape(n, stations, width)
        mine = energies.at[iteration, chan]
        other_chans(lambda c: remote(mine, mine, PAIR + iteration, {"chan": c}))
        wait_all(energies.at[iteration], nchan - 1, recv_sem.at[PAIR + iteration])
        chip_sum[iteration] = jnp.sum(energies[iteration], axis=0)
        other_stations(
            lambda s: remote(
                chip_sum.at[iteration, s], sums.at[iteration, stn], SUMS + iteration, {"stn": s}
            )
        )
        sums[iteration, stn] = chip_sum[iteration, stn]
        wait_all(sums.at[iteration], n - 1, recv_sem.at[SUMS + iteration])
        scale = -(2.0 / half) / half
        block = scale * jnp.sum(sums[iteration], axis=0)
        if iteration < ITERS - 1:
            gathered[iteration, stn] = block
            part = gathered.at[iteration, stn]
            other_stations(lambda s: remote(part, part, GATHER + iteration, {"stn": s}))
            wait_all(gathered.at[iteration], n - 1, recv_sem.at[GATHER + iteration])
            gradient = gathered[iteration].reshape(everyone, width)
            spread = jnp.sqrt(jnp.sum(gradient * gradient, keepdims=True) / (everyone * half) + 1e-06)
            held = gains if iteration == 0 else current
            current[...] = held[...] - steps * (gradient / spread)
        else:
            norms[stn] = jnp.sum(block * block, axis=0, keepdims=True)
            part = norms.at[stn]
            other_stations(lambda s: remote(part, part, GATHER + iteration, {"stn": s}))
            own = current[pl.ds(pl.multiple_of(stn * stations, stations), stations), :]
            wait_all(norms, n - 1, recv_sem.at[GATHER + iteration])
            total = jnp.sum(jnp.sum(norms[...], axis=0), keepdims=True)
            spread = jnp.sqrt(total / (everyone * half) + 1e-06)
            descent = block / spread
            result_ref[0] = own - steps * descent
            result_ref[1] = descent

    wait_all(id_rows, n - 1, send_sem.at[IDS])
    wait_all(resp_send, n - 1, send_sem.at[RESP])
    for chunk in range(chunks):
        part = volt_send.at[pl.ds(0, n - 1), chunk_rows[chunk]]
        pltpu.make_async_copy(part, part, send_sem.at[VOLT + chunk]).wait()
    for iteration in range(ITERS):
        wait_all(energies.at[iteration], nchan - 1, send_sem.at[PAIR + iteration])
        wait_all(sums.at[iteration], n - 1, send_sem.at[SUMS + iteration])
        last = gathered.at[iteration] if iteration < ITERS - 1 else norms
        wait_all(last, n - 1, send_sem.at[GATHER + iteration])


def shards(n, nchan, voltages, response, start_gains, step_sizes, station_ids, baseline_flags):
    stations, width = voltages.shape[0], voltages.shape[3]
    samples = voltages.shape[1] * voltages.shape[2]
    everyone = stations * n
    spd = samples // n
    half = width // 2
    f32, bf16 = jnp.float32, jnp.bfloat16
    hbm = pl.BlockSpec(memory_space=pltpu.HBM)
    vmem = pl.BlockSpec(memory_space=pltpu.VMEM)
    block = (n, spd * stations, width)
    scratch = [
        ((stations, samples, width), bf16),
        ((stations, samples, width), bf16),
        ((everyone, width), f32),
        ((everyone, everyone), jnp.int32),
        ((stations * samples, width), f32),
        ((stations * samples, width), f32),
        (block, bf16),
        (block, bf16),
        (block, bf16),
        (block, bf16),
        ((n, 1, everyone), jnp.int32),
        ((everyone, everyone), f32),
        ((spd, everyone, width), f32),
        ((spd, everyone, width), f32),
        ((spd, 2 * everyone, width), bf16),
        ((spd, everyone, 2 * everyone), f32),
        ((spd, everyone, 2 * everyone), f32),
        ((ITERS, nchan, n, stations, width), f32),
        ((ITERS, n, stations, width), f32),
        ((ITERS, n, stations, width), f32),
        ((ITERS - 1, n, stations, width), f32),
        ((n, 1, width), f32),
        ((everyone, width), f32),
        ((half,), f32),
    ]
    result = pl.pallas_call(
        functools.partial(kernel, n, nchan, stations, samples),
        out_shape=jax.ShapeDtypeStruct((2, stations, width), f32),
        in_specs=[hbm] * 6,
        out_specs=vmem,
        scratch_shapes=[pltpu.VMEM(shape, dtype) for shape, dtype in scratch]
        + [pltpu.SMEM((stations,), jnp.int32), pltpu.SemaphoreType.DMA((6,)), pltpu.SemaphoreType.DMA((GROUPS,)), pltpu.SemaphoreType.DMA((GROUPS,))],
        compiler_params=pltpu.CompilerParams(
            collective_id=0, has_side_effects=True, vmem_limit_bytes=64 * 1024 * 1024
        ),
    )(
        voltages.reshape(stations, samples, width),
        response.reshape(stations, samples, width),
        start_gains, step_sizes, station_ids, baseline_flags,
    )
    return result[0], result[1]


def solution(mesh):
    placed = (P("stn", "chan", None, None), P("stn", "chan", None, None), P(), P(), P("stn"), P())
    return jax.shard_map(
        functools.partial(shards, mesh.shape["stn"], mesh.shape["chan"]),
        mesh=mesh,
        in_specs=placed,
        out_specs=(P("stn", None), P("stn", None)),
        check_vma=False,
    )
```

```python
import functools

import jax
import jax.numpy as jnp
from jax import lax
from jax.experimental import pallas as pl
from jax.experimental.pallas import tpu as pltpu
from jax.sharding import PartitionSpec as P

ITERS = 2
MESH = pl.DeviceIdType.MESH
IDS, RESP, VOLT, PAIR = 0, 1, 2, 4
SUMS = PAIR + ITERS
GATHER = SUMS + ITERS
GROUPS = GATHER + ITERS


def dot_last(left, right):
    return lax.dot_general(left, right, (((1,), (1,)), ((), ())), preferred_element_type=jnp.float32)


def dot(left, right):
    return lax.dot_general(left, right, (((1,), (0,)), ((), ())), preferred_element_type=jnp.float32)


def kernel(
    n, nchan, stations, samples,
    volt_any, resp_any, gains_any, steps_any, ids_any, flags_any,
    result_ref,
    volt_in, resp_in, gains, flags, wide_volt, wide_resp,
    volt_send, resp_send, volt_recv, resp_recv, id_rows,
    weight, a_float, a_swap, applied, observed, predicted,
    energies, chip_sum, sums, gathered, norms, current, steps_ref, ids_ref,
    in_sem, send_sem, recv_sem,
):
    everyone = n * stations
    spd = samples // n
    width = volt_in.shape[2]
    half = width // 2
    stn = lax.axis_index("stn")
    chan = lax.axis_index("chan")

    def each(first, stop, body):
        if stop - first <= 16:
            quarter = max(stop // 4, 1)
            for k in sorted(range(first, stop), key=lambda k: (k % quarter, (2, 1, 3, 0).index(k // quarter % 4))):
                body(k)
        else:
            lax.fori_loop(first, stop, lambda k, carry: (body(k), carry)[1], 0)

    def other_stations(body):
        each(1, n, lambda k: body(lax.rem(stn + k, n)))

    def other_chans(body):
        for c in range(1, nchan):
            body(lax.rem(chan + c, nchan))

    loads = [
        pltpu.make_async_copy(src, dst, in_sem.at[i])
        for i, (src, dst) in enumerate(
            (
                (ids_any, ids_ref), (resp_any, resp_in), (volt_any, volt_in),
                (flags_any, flags), (gains_any, gains), (steps_any, steps_ref),
            )
        )
    ]
    for load in loads:
        load.start()

    barrier = pltpu.get_barrier_semaphore()

    def greet(device):
        pl.semaphore_signal(barrier, inc=1, device_id=device, device_id_type=MESH)

    other_stations(lambda s: greet({"stn": s}))
    other_chans(lambda c: greet({"chan": c}))

    def wait_all(buffer, count, sem):
        part = buffer.at[pl.ds(0, count)]
        pltpu.make_async_copy(part, part, sem).wait()

    loads[0].wait()
    lane = lax.broadcasted_iota(jnp.int32, (1, everyone), 1)
    own_row = jnp.zeros((1, everyone), jnp.int32)
    for j in range(stations):
        own_row = jnp.where(lane == stn * stations + j, ids_ref[j], own_row)
    id_rows[stn] = own_row

    loads[1].wait()
    wide_resp[...] = resp_in[...].astype(jnp.float32).reshape(stations * samples, width)

    def pack(wide, send, dst, pairs):
        for pair in pairs:
            first = dst * spd + 2 * pair
            both = jnp.concatenate(
                [wide[pl.ds(first + j, stations, stride=samples), :] for j in range(2)], axis=0
            )
            send[dst, pl.ds(2 * pair * stations, 2 * stations), :] = both.astype(jnp.bfloat16)

    def remote(src, dst_ref, group, device):
        pltpu.make_async_remote_copy(
            src_ref=src, dst_ref=dst_ref, send_sem=send_sem.at[group],
            recv_sem=recv_sem.at[group], device_id=device, device_id_type=MESH,
        ).start()

    pairs = spd // 2
    chunks = 2 if pairs > 1 else 1
    chunk_pairs = [range(pairs - 1), range(pairs - 1, pairs)][2 - chunks:]
    chunk_rows = [
        pl.ds(2 * part.start * stations, 2 * len(part) * stations) for part in chunk_pairs
    ]

    pl.semaphore_wait(barrier, n + nchan - 2)

    def send_resp(dst):
        remote(id_rows.at[stn], id_rows.at[stn], IDS, {"stn": dst})
        pack(wide_resp, resp_send, dst, range(pairs))
        remote(resp_send.at[dst], resp_recv.at[stn], RESP, {"stn": dst})

    other_stations(send_resp)
    loads[2].wait()
    wide_volt[...] = volt_in[...].astype(jnp.float32).reshape(stations * samples, width)
    for chunk in range(chunks):

        def send_volt(dst, chunk=chunk):
            pack(wide_volt, volt_send, dst, chunk_pairs[chunk])
            part = chunk_rows[chunk]
            remote(volt_send.at[dst, part], volt_recv.at[stn, part], VOLT + chunk, {"stn": dst})

        other_stations(send_volt)
    pack(wide_resp, resp_send, stn, range(pairs))
    resp_recv[stn] = resp_send[stn]
    pack(wide_volt, volt_send, stn, range(pairs))
    volt_recv[stn] = volt_send[stn]

    loads[3].wait()
    flag = flags[...].astype(jnp.float32)
    mutual = (flag * flag.T).astype(jnp.bfloat16)
    wait_all(id_rows, n - 1, recv_sem.at[IDS])
    all_ids = jnp.sum(id_rows[...], axis=0)
    row = lax.broadcasted_iota(jnp.int32, (everyone, everyone), 0)
    column = lax.broadcasted_iota(jnp.int32, (everyone, everyone), 1)
    one_hot = (row == all_ids).astype(jnp.float32).astype(jnp.bfloat16)
    picked = dot(mutual, one_hot).T.astype(jnp.bfloat16)
    weight[...] = jnp.where(row == column, 0.0, dot(picked, one_hot))

    def unpack(recv, pair):
        block = recv[:, pl.ds(2 * pair * stations, 2 * stations), :].astype(jnp.float32)
        block = block.reshape(n, 2, stations, width)
        return [block[:, j].reshape(everyone, width) for j in range(2)]

    sign = jnp.where(lax.broadcasted_iota(jnp.int32, (1, width), 1) < half, -1.0, 1.0)
    loads[4].wait()
    loads[5].wait()
    steps = steps_ref[...].reshape(1, half)
    steps = jnp.concatenate([steps, steps], axis=1)

    def predict(t, gain_both, gain_turn):
        a = a_float[t]
        turned = gain_both * a + gain_turn * a_swap[t]
        applied[t, pl.ds(0, everyone), :] = turned.astype(jnp.bfloat16)
        applied[t, pl.ds(everyone, everyone), :] = (sign * pltpu.roll(turned, half, 1)).astype(jnp.bfloat16)
        return dot_last(applied[t, pl.ds(0, everyone), :], applied[t])

    def gain_parts(gain):
        swapped = pltpu.roll(gain, half, 1)
        left = sign < 0.0
        return jnp.where(left, gain, swapped), jnp.where(left, -swapped, gain)

    wait_all(resp_recv, n - 1, recv_sem.at[RESP])
    gain_both, gain_turn = gain_parts(gains[...])
    for pair in range(spd // 2):
        for j, a in enumerate(unpack(resp_recv, pair)):
            t = 2 * pair + j
            a_float[t] = a
            a_swap[t] = pltpu.roll(a, half, 1)
            predicted[t] = predict(t, gain_both, gain_turn)

    def accumulate(t, left_over, totals):
        residual = jnp.concatenate(
            [
                (weight[...] * left_over[:, :everyone]).astype(jnp.bfloat16),
                (weight[...] * left_over[:, everyone:]).astype(jnp.bfloat16),
            ],
            axis=1,
        )
        hidden = dot(residual, applied[t])
        return totals[0] + a_float[t] * hidden, totals[1] + a_swap[t] * hidden

    def volt_chunk(chunk):
        part = volt_recv.at[pl.ds(0, n - 1), chunk_rows[chunk]]
        return pltpu.make_async_copy(part, part, recv_sem.at[VOLT + chunk])

    for iteration in range(ITERS):
        totals = (jnp.zeros((everyone, width), jnp.float32), jnp.zeros((everyone, width), jnp.float32))
        if iteration == 0:
            for chunk in range(chunks):
                volt_chunk(chunk).wait()
                for pair in chunk_pairs[chunk]:
                    for j, x in enumerate(unpack(volt_recv, pair)):
                        t = 2 * pair + j
                        mine = x.astype(jnp.bfloat16)
                        turned = (sign * pltpu.roll(x, half, 1)).astype(jnp.bfloat16)
                        seen = dot_last(mine, jnp.concatenate([mine, turned], axis=0))
                        observed[t] = seen
                        totals = accumulate(t, seen - predicted[t], totals)
        else:
            gain_both, gain_turn = gain_parts(current[...])
            left_over = observed[0] - predict(0, gain_both, gain_turn)
            for t in range(spd):
                held_over = left_over
                if t + 1 < spd:
                    left_over = observed[t + 1] - predict(t + 1, gain_both, gain_turn)
                totals = accumulate(t, held_over, totals)
        direct, crossed = totals
        energy = jnp.where(
            sign < 0.0,
            direct + pltpu.roll(direct, half, 1),
            crossed - pltpu.roll(crossed, half, 1),
        )
        energies[iteration, chan] = energy.reshape(n, stations, width)
        mine = energies.at[iteration, chan]
        other_chans(lambda c: remote(mine, mine, PAIR + iteration, {"chan": c}))
        wait_all(energies.at[iteration], nchan - 1, recv_sem.at[PAIR + iteration])
        chip_sum[iteration] = jnp.sum(energies[iteration], axis=0)
        other_stations(
            lambda s: remote(
                chip_sum.at[iteration, s], sums.at[iteration, stn], SUMS + iteration, {"stn": s}
            )
        )
        sums[iteration, stn] = chip_sum[iteration, stn]
        wait_all(sums.at[iteration], n - 1, recv_sem.at[SUMS + iteration])
        scale = -(2.0 / half) / half
        block = scale * jnp.sum(sums[iteration], axis=0)
        if iteration < ITERS - 1:
            gathered[iteration, stn] = block
            part = gathered.at[iteration, stn]
            other_stations(lambda s: remote(part, part, GATHER + iteration, {"stn": s}))
            wait_all(gathered.at[iteration], n - 1, recv_sem.at[GATHER + iteration])
            gradient = gathered[iteration].reshape(everyone, width)
            spread = jnp.sqrt(jnp.sum(gradient * gradient, keepdims=True) / (everyone * half) + 1e-06)
            held = gains if iteration == 0 else current
            current[...] = held[...] - steps * (gradient / spread)
        else:
            norms[stn] = jnp.sum(block * block, axis=0, keepdims=True)
            part = norms.at[stn]
            other_stations(lambda s: remote(part, part, GATHER + iteration, {"stn": s}))
            own = current[pl.ds(pl.multiple_of(stn * stations, stations), stations), :]
            wait_all(norms, n - 1, recv_sem.at[GATHER + iteration])
            total = jnp.sum(jnp.sum(norms[...], axis=0), keepdims=True)
            spread = jnp.sqrt(total / (everyone * half) + 1e-06)
            descent = block / spread
            result_ref[0] = own - steps * descent
            result_ref[1] = descent

    wait_all(id_rows, n - 1, send_sem.at[IDS])
    wait_all(resp_send, n - 1, send_sem.at[RESP])
    for chunk in range(chunks):
        part = volt_send.at[pl.ds(0, n - 1), chunk_rows[chunk]]
        pltpu.make_async_copy(part, part, send_sem.at[VOLT + chunk]).wait()
    for iteration in range(ITERS):
        wait_all(energies.at[iteration], nchan - 1, send_sem.at[PAIR + iteration])
        wait_all(sums.at[iteration], n - 1, send_sem.at[SUMS + iteration])
        last = gathered.at[iteration] if iteration < ITERS - 1 else norms
        wait_all(last, n - 1, send_sem.at[GATHER + iteration])


def shards(n, nchan, voltages, response, start_gains, step_sizes, station_ids, baseline_flags):
    stations, width = voltages.shape[0], voltages.shape[3]
    samples = voltages.shape[1] * voltages.shape[2]
    everyone = stations * n
    spd = samples // n
    half = width // 2
    f32, bf16 = jnp.float32, jnp.bfloat16
    hbm = pl.BlockSpec(memory_space=pltpu.HBM)
    vmem = pl.BlockSpec(memory_space=pltpu.VMEM)
    block = (n, spd * stations, width)
    scratch = [
        ((stations, samples, width), bf16),
        ((stations, samples, width), bf16),
        ((everyone, width), f32),
        ((everyone, everyone), jnp.int32),
        ((stations * samples, width), f32),
        ((stations * samples, width), f32),
        (block, bf16),
        (block, bf16),
        (block, bf16),
        (block, bf16),
        ((n, 1, everyone), jnp.int32),
        ((everyone, everyone), f32),
        ((spd, everyone, width), f32),
        ((spd, everyone, width), f32),
        ((spd, 2 * everyone, width), bf16),
        ((spd, everyone, 2 * everyone), f32),
        ((spd, everyone, 2 * everyone), f32),
        ((ITERS, nchan, n, stations, width), f32),
        ((ITERS, n, stations, width), f32),
        ((ITERS, n, stations, width), f32),
        ((ITERS - 1, n, stations, width), f32),
        ((n, 1, width), f32),
        ((everyone, width), f32),
        ((half,), f32),
    ]
    result = pl.pallas_call(
        functools.partial(kernel, n, nchan, stations, samples),
        out_shape=jax.ShapeDtypeStruct((2, stations, width), f32),
        in_specs=[hbm] * 6,
        out_specs=vmem,
        scratch_shapes=[pltpu.VMEM(shape, dtype) for shape, dtype in scratch]
        + [pltpu.SMEM((stations,), jnp.int32), pltpu.SemaphoreType.DMA((6,)), pltpu.SemaphoreType.DMA((GROUPS,)), pltpu.SemaphoreType.DMA((GROUPS,))],
        compiler_params=pltpu.CompilerParams(
            collective_id=0, has_side_effects=True, vmem_limit_bytes=64 * 1024 * 1024
        ),
    )(
        voltages.reshape(stations, samples, width),
        response.reshape(stations, samples, width),
        start_gains, step_sizes, station_ids, baseline_flags,
    )
    return result[0], result[1]


def solution(mesh):
    placed = (P("stn", "chan", None, None), P("stn", "chan", None, None), P(), P(), P("stn"), P())
    return jax.shard_map(
        functools.partial(shards, mesh.shape["stn"], mesh.shape["chan"]),
        mesh=mesh,
        in_specs=placed,
        out_specs=(P("stn", None), P("stn", None)),
        check_vma=False,
    )
```

```python
import functools

import jax
import jax.numpy as jnp
from jax import lax
from jax.experimental import pallas as pl
from jax.experimental.pallas import tpu as pltpu
from jax.sharding import PartitionSpec as P

ITERS = 2
MESH = pl.DeviceIdType.MESH
IDS, RESP, VOLT, PAIR = 0, 1, 2, 4
SUMS = PAIR + ITERS
GATHER = SUMS + ITERS
GROUPS = GATHER + ITERS


def dot_last(left, right):
    return lax.dot_general(left, right, (((1,), (1,)), ((), ())), preferred_element_type=jnp.float32)


def dot(left, right):
    return lax.dot_general(left, right, (((1,), (0,)), ((), ())), preferred_element_type=jnp.float32)


def kernel(
    n, nchan, stations, samples,
    volt_any, resp_any, gains_any, steps_any, ids_any, flags_any,
    result_ref,
    volt_in, resp_in, gains, flags, wide_volt, wide_resp,
    volt_send, resp_send, volt_recv, resp_recv, id_rows,
    weight, a_float, a_swap, applied, observed, predicted,
    energies, chip_sum, sums, gathered, norms, current, steps_ref, ids_ref,
    in_sem, send_sem, recv_sem,
):
    everyone = n * stations
    spd = samples // n
    width = volt_in.shape[2]
    half = width // 2
    stn = lax.axis_index("stn")
    chan = lax.axis_index("chan")

    def each(first, stop, body):
        if stop - first <= 16:
            quarter = max(stop // 4, 1)
            for k in sorted(range(first, stop), key=lambda k: (k % quarter, (2, 1, 3, 0).index(k // quarter % 4))):
                body(k)
        else:
            lax.fori_loop(first, stop, lambda k, carry: (body(k), carry)[1], 0)

    def other_stations(body):
        each(1, n, lambda k: body(lax.rem(stn + k, n)))

    def other_chans(body):
        for c in range(1, nchan):
            body(lax.rem(chan + c, nchan))

    barrier = pltpu.get_barrier_semaphore()

    def greet(device):
        pl.semaphore_signal(barrier, inc=1, device_id=device, device_id_type=MESH)

    other_stations(lambda s: greet({"stn": s}))
    other_chans(lambda c: greet({"chan": c}))

    loads = [
        pltpu.make_async_copy(src, dst, in_sem.at[i])
        for i, (src, dst) in enumerate(
            (
                (ids_any, ids_ref), (resp_any, resp_in), (volt_any, volt_in),
                (flags_any, flags), (gains_any, gains), (steps_any, steps_ref),
            )
        )
    ]
    for load in loads:
        load.start()

    def wait_all(buffer, count, sem):
        part = buffer.at[pl.ds(0, count)]
        pltpu.make_async_copy(part, part, sem).wait()

    loads[0].wait()
    lane = lax.broadcasted_iota(jnp.int32, (1, everyone), 1)
    own_row = jnp.zeros((1, everyone), jnp.int32)
    for j in range(stations):
        own_row = jnp.where(lane == stn * stations + j, ids_ref[j], own_row)
    id_rows[stn] = own_row

    loads[1].wait()
    wide_resp[...] = resp_in[...].astype(jnp.float32).reshape(stations * samples, width)

    def pack(wide, send, dst, pairs):
        for pair in pairs:
            first = dst * spd + 2 * pair
            both = jnp.concatenate(
                [wide[pl.ds(first + j, stations, stride=samples), :] for j in range(2)], axis=0
            )
            send[dst, pl.ds(2 * pair * stations, 2 * stations), :] = both.astype(jnp.bfloat16)

    def remote(src, dst_ref, group, device):
        pltpu.make_async_remote_copy(
            src_ref=src, dst_ref=dst_ref, send_sem=send_sem.at[group],
            recv_sem=recv_sem.at[group], device_id=device, device_id_type=MESH,
        ).start()

    pairs = spd // 2
    chunks = 2 if pairs > 1 else 1
    chunk_pairs = [range(pairs - 1), range(pairs - 1, pairs)][2 - chunks:]
    chunk_rows = [
        pl.ds(2 * part.start * stations, 2 * len(part) * stations) for part in chunk_pairs
    ]

    pl.semaphore_wait(barrier, n + nchan - 2)

    def send_resp(dst):
        pack(wide_resp, resp_send, dst, range(pairs))
        remote(resp_send.at[dst], resp_recv.at[stn], RESP, {"stn": dst})

    other_stations(send_resp)
    other_stations(lambda s: remote(id_rows.at[stn], id_rows.at[stn], IDS, {"stn": s}))
    loads[2].wait()
    wide_volt[...] = volt_in[...].astype(jnp.float32).reshape(stations * samples, width)
    for chunk in range(chunks):

        def send_volt(dst, chunk=chunk):
            pack(wide_volt, volt_send, dst, chunk_pairs[chunk])
            part = chunk_rows[chunk]
            remote(volt_send.at[dst, part], volt_recv.at[stn, part], VOLT + chunk, {"stn": dst})

        other_stations(send_volt)
    pack(wide_resp, resp_send, stn, range(pairs))
    resp_recv[stn] = resp_send[stn]
    pack(wide_volt, volt_send, stn, range(pairs))
    volt_recv[stn] = volt_send[stn]

    loads[3].wait()
    flag = flags[...].astype(jnp.float32)
    mutual = (flag * flag.T).astype(jnp.bfloat16)
    wait_all(id_rows, n - 1, recv_sem.at[IDS])
    all_ids = jnp.sum(id_rows[...], axis=0)
    row = lax.broadcasted_iota(jnp.int32, (everyone, everyone), 0)
    column = lax.broadcasted_iota(jnp.int32, (everyone, everyone), 1)
    one_hot = (row == all_ids).astype(jnp.float32).astype(jnp.bfloat16)
    picked = dot(mutual, one_hot).T.astype(jnp.bfloat16)
    weight[...] = jnp.where(row == column, 0.0, dot(picked, one_hot))

    def unpack(recv, pair):
        block = recv[:, pl.ds(2 * pair * stations, 2 * stations), :].astype(jnp.float32)
        block = block.reshape(n, 2, stations, width)
        return [block[:, j].reshape(everyone, width) for j in range(2)]

    sign = jnp.where(lax.broadcasted_iota(jnp.int32, (1, width), 1) < half, -1.0, 1.0)
    loads[4].wait()
    loads[5].wait()
    steps = steps_ref[...].reshape(1, half)
    steps = jnp.concatenate([steps, steps], axis=1)

    def predict(t, gain_both, gain_turn):
        a = a_float[t]
        turned = gain_both * a + gain_turn * a_swap[t]
        applied[t, pl.ds(0, everyone), :] = turned.astype(jnp.bfloat16)
        applied[t, pl.ds(everyone, everyone), :] = (sign * pltpu.roll(turned, half, 1)).astype(jnp.bfloat16)
        return dot_last(applied[t, pl.ds(0, everyone), :], applied[t])

    def gain_parts(gain):
        swapped = pltpu.roll(gain, half, 1)
        left = sign < 0.0
        return jnp.where(left, gain, swapped), jnp.where(left, -swapped, gain)

    wait_all(resp_recv, n - 1, recv_sem.at[RESP])
    gain_both, gain_turn = gain_parts(gains[...])
    for pair in range(spd // 2):
        for j, a in enumerate(unpack(resp_recv, pair)):
            t = 2 * pair + j
            a_float[t] = a
            a_swap[t] = pltpu.roll(a, half, 1)
            predicted[t] = predict(t, gain_both, gain_turn)

    def accumulate(t, left_over, totals):
        residual = jnp.concatenate(
            [
                (weight[...] * left_over[:, :everyone]).astype(jnp.bfloat16),
                (weight[...] * left_over[:, everyone:]).astype(jnp.bfloat16),
            ],
            axis=1,
        )
        hidden = dot(residual, applied[t])
        return totals[0] + a_float[t] * hidden, totals[1] + a_swap[t] * hidden

    def volt_chunk(chunk):
        part = volt_recv.at[pl.ds(0, n - 1), chunk_rows[chunk]]
        return pltpu.make_async_copy(part, part, recv_sem.at[VOLT + chunk])

    for iteration in range(ITERS):
        totals = (jnp.zeros((everyone, width), jnp.float32), jnp.zeros((everyone, width), jnp.float32))
        if iteration == 0:
            for chunk in range(chunks):
                volt_chunk(chunk).wait()
                for pair in chunk_pairs[chunk]:
                    for j, x in enumerate(unpack(volt_recv, pair)):
                        t = 2 * pair + j
                        mine = x.astype(jnp.bfloat16)
                        turned = (sign * pltpu.roll(x, half, 1)).astype(jnp.bfloat16)
                        seen = dot_last(mine, jnp.concatenate([mine, turned], axis=0))
                        observed[t] = seen
                        totals = accumulate(t, seen - predicted[t], totals)
        else:
            gain_both, gain_turn = gain_parts(current[...])
            left_over = observed[0] - predict(0, gain_both, gain_turn)
            for t in range(spd):
                held_over = left_over
                if t + 1 < spd:
                    left_over = observed[t + 1] - predict(t + 1, gain_both, gain_turn)
                totals = accumulate(t, held_over, totals)
        direct, crossed = totals
        energy = jnp.where(
            sign < 0.0,
            direct + pltpu.roll(direct, half, 1),
            crossed - pltpu.roll(crossed, half, 1),
        )
        energies[iteration, chan] = energy.reshape(n, stations, width)
        mine = energies.at[iteration, chan]
        other_chans(lambda c: remote(mine, mine, PAIR + iteration, {"chan": c}))
        wait_all(energies.at[iteration], nchan - 1, recv_sem.at[PAIR + iteration])
        chip_sum[iteration] = jnp.sum(energies[iteration], axis=0)
        other_stations(
            lambda s: remote(
                chip_sum.at[iteration, s], sums.at[iteration, stn], SUMS + iteration, {"stn": s}
            )
        )
        sums[iteration, stn] = chip_sum[iteration, stn]
        wait_all(sums.at[iteration], n - 1, recv_sem.at[SUMS + iteration])
        scale = -(2.0 / half) / half
        block = scale * jnp.sum(sums[iteration], axis=0)
        if iteration < ITERS - 1:
            gathered[iteration, stn] = block
            part = gathered.at[iteration, stn]
            other_stations(lambda s: remote(part, part, GATHER + iteration, {"stn": s}))
            wait_all(gathered.at[iteration], n - 1, recv_sem.at[GATHER + iteration])
            gradient = gathered[iteration].reshape(everyone, width)
            spread = jnp.sqrt(jnp.sum(gradient * gradient, keepdims=True) / (everyone * half) + 1e-06)
            held = gains if iteration == 0 else current
            current[...] = held[...] - steps * (gradient / spread)
        else:
            norms[stn] = jnp.sum(block * block, axis=0, keepdims=True)
            part = norms.at[stn]
            other_stations(lambda s: remote(part, part, GATHER + iteration, {"stn": s}))
            own = current[pl.ds(pl.multiple_of(stn * stations, stations), stations), :]
            wait_all(norms, n - 1, recv_sem.at[GATHER + iteration])
            total = jnp.sum(jnp.sum(norms[...], axis=0), keepdims=True)
            spread = jnp.sqrt(total / (everyone * half) + 1e-06)
            descent = block / spread
            result_ref[0] = own - steps * descent
            result_ref[1] = descent

    wait_all(id_rows, n - 1, send_sem.at[IDS])
    wait_all(resp_send, n - 1, send_sem.at[RESP])
    for chunk in range(chunks):
        part = volt_send.at[pl.ds(0, n - 1), chunk_rows[chunk]]
        pltpu.make_async_copy(part, part, send_sem.at[VOLT + chunk]).wait()
    for iteration in range(ITERS):
        wait_all(energies.at[iteration], nchan - 1, send_sem.at[PAIR + iteration])
        wait_all(sums.at[iteration], n - 1, send_sem.at[SUMS + iteration])
        last = gathered.at[iteration] if iteration < ITERS - 1 else norms
        wait_all(last, n - 1, send_sem.at[GATHER + iteration])


def shards(n, nchan, voltages, response, start_gains, step_sizes, station_ids, baseline_flags):
    stations, width = voltages.shape[0], voltages.shape[3]
    samples = voltages.shape[1] * voltages.shape[2]
    everyone = stations * n
    spd = samples // n
    half = width // 2
    f32, bf16 = jnp.float32, jnp.bfloat16
    hbm = pl.BlockSpec(memory_space=pltpu.HBM)
    vmem = pl.BlockSpec(memory_space=pltpu.VMEM)
    block = (n, spd * stations, width)
    scratch = [
        ((stations, samples, width), bf16),
        ((stations, samples, width), bf16),
        ((everyone, width), f32),
        ((everyone, everyone), jnp.int32),
        ((stations * samples, width), f32),
        ((stations * samples, width), f32),
        (block, bf16),
        (block, bf16),
        (block, bf16),
        (block, bf16),
        ((n, 1, everyone), jnp.int32),
        ((everyone, everyone), f32),
        ((spd, everyone, width), f32),
        ((spd, everyone, width), f32),
        ((spd, 2 * everyone, width), bf16),
        ((spd, everyone, 2 * everyone), f32),
        ((spd, everyone, 2 * everyone), f32),
        ((ITERS, nchan, n, stations, width), f32),
        ((ITERS, n, stations, width), f32),
        ((ITERS, n, stations, width), f32),
        ((ITERS - 1, n, stations, width), f32),
        ((n, 1, width), f32),
        ((everyone, width), f32),
        ((half,), f32),
    ]
    result = pl.pallas_call(
        functools.partial(kernel, n, nchan, stations, samples),
        out_shape=jax.ShapeDtypeStruct((2, stations, width), f32),
        in_specs=[hbm] * 6,
        out_specs=vmem,
        scratch_shapes=[pltpu.VMEM(shape, dtype) for shape, dtype in scratch]
        + [pltpu.SMEM((stations,), jnp.int32), pltpu.SemaphoreType.DMA((6,)), pltpu.SemaphoreType.DMA((GROUPS,)), pltpu.SemaphoreType.DMA((GROUPS,))],
        compiler_params=pltpu.CompilerParams(
            collective_id=0, has_side_effects=True, vmem_limit_bytes=64 * 1024 * 1024
        ),
    )(
        voltages.reshape(stations, samples, width),
        response.reshape(stations, samples, width),
        start_gains, step_sizes, station_ids, baseline_flags,
    )
    return result[0], result[1]


def solution(mesh):
    placed = (P("stn", "chan", None, None), P("stn", "chan", None, None), P(), P(), P("stn"), P())
    return jax.shard_map(
        functools.partial(shards, mesh.shape["stn"], mesh.shape["chan"]),
        mesh=mesh,
        in_specs=placed,
        out_specs=(P("stn", None), P("stn", None)),
        check_vma=False,
    )
```

```python
import functools

import jax
import jax.numpy as jnp
from jax import lax
from jax.experimental import pallas as pl
from jax.experimental.pallas import tpu as pltpu
from jax.sharding import PartitionSpec as P

ITERS = 2
MESH = pl.DeviceIdType.MESH
IDS, RESP, VOLT, PAIR = 0, 1, 2, 4
SUMS = PAIR + ITERS
GATHER = SUMS + ITERS
GROUPS = GATHER + ITERS


def dot_last(left, right):
    return lax.dot_general(left, right, (((1,), (1,)), ((), ())), preferred_element_type=jnp.float32)


def dot(left, right):
    return lax.dot_general(left, right, (((1,), (0,)), ((), ())), preferred_element_type=jnp.float32)


def kernel(
    n, nchan, stations, samples,
    volt_any, resp_any, gains_any, steps_any, ids_any, flags_any,
    result_ref,
    volt_in, resp_in, gains, flags, wide_volt, wide_resp,
    volt_send, resp_send, volt_recv, resp_recv, id_rows,
    weight, a_float, a_swap, applied, observed, predicted,
    energies, chip_sum, sums, gathered, norms, current, steps_ref, ids_ref,
    in_sem, send_sem, recv_sem,
):
    everyone = n * stations
    spd = samples // n
    width = volt_in.shape[2]
    half = width // 2
    pitch = samples + 8
    stn = lax.axis_index("stn")
    chan = lax.axis_index("chan")

    def each(first, stop, body):
        if stop - first <= 16:
            quarter = max(stop // 4, 1)
            for k in sorted(range(first, stop), key=lambda k: (k % quarter, (2, 1, 3, 0).index(k // quarter % 4))):
                body(k)
        else:
            lax.fori_loop(first, stop, lambda k, carry: (body(k), carry)[1], 0)

    def other_stations(body):
        each(1, n, lambda k: body(lax.rem(stn + k, n)))

    def other_chans(body):
        for c in range(1, nchan):
            body(lax.rem(chan + c, nchan))

    barrier = pltpu.get_barrier_semaphore()

    def greet(device):
        pl.semaphore_signal(barrier, inc=1, device_id=device, device_id_type=MESH)

    other_stations(lambda s: greet({"stn": s}))
    other_chans(lambda c: greet({"chan": c}))

    loads = [
        pltpu.make_async_copy(src, dst, in_sem.at[i])
        for i, (src, dst) in enumerate(
            (
                (ids_any, ids_ref), (resp_any, resp_in), (volt_any, volt_in),
                (flags_any, flags), (gains_any, gains), (steps_any, steps_ref),
            )
        )
    ]
    for load in loads:
        load.start()

    def wait_all(buffer, count, sem):
        part = buffer.at[pl.ds(0, count)]
        pltpu.make_async_copy(part, part, sem).wait()

    loads[0].wait()
    lane = lax.broadcasted_iota(jnp.int32, (1, everyone), 1)
    own_row = jnp.zeros((1, everyone), jnp.int32)
    for j in range(stations):
        own_row = jnp.where(lane == stn * stations + j, ids_ref[j], own_row)
    id_rows[stn] = own_row

    loads[1].wait()
    for p in range(stations):
        wide_resp[pl.ds(p * pitch, samples), :] = resp_in[p].astype(jnp.float32)

    def pack(wide, send, dst, pairs):
        for pair in pairs:
            first = dst * spd + 2 * pair
            both = jnp.concatenate(
                [wide[pl.ds(first + j, stations, stride=pitch), :] for j in range(2)], axis=0
            )
            send[dst, pl.ds(2 * pair * stations, 2 * stations), :] = both.astype(jnp.bfloat16)

    def remote(src, dst_ref, group, device):
        pltpu.make_async_remote_copy(
            src_ref=src, dst_ref=dst_ref, send_sem=send_sem.at[group],
            recv_sem=recv_sem.at[group], device_id=device, device_id_type=MESH,
        ).start()

    pairs = spd // 2
    chunks = 2 if pairs > 1 else 1
    chunk_pairs = [range(pairs - 1), range(pairs - 1, pairs)][2 - chunks:]
    chunk_rows = [
        pl.ds(2 * part.start * stations, 2 * len(part) * stations) for part in chunk_pairs
    ]

    pl.semaphore_wait(barrier, n + nchan - 2)

    def send_resp(dst):
        pack(wide_resp, resp_send, dst, range(pairs))
        remote(resp_send.at[dst], resp_recv.at[stn], RESP, {"stn": dst})

    other_stations(send_resp)
    other_stations(lambda s: remote(id_rows.at[stn], id_rows.at[stn], IDS, {"stn": s}))
    loads[2].wait()
    for p in range(stations):
        wide_volt[pl.ds(p * pitch, samples), :] = volt_in[p].astype(jnp.float32)
    for chunk in range(chunks):

        def send_volt(dst, chunk=chunk):
            pack(wide_volt, volt_send, dst, chunk_pairs[chunk])
            part = chunk_rows[chunk]
            remote(volt_send.at[dst, part], volt_recv.at[stn, part], VOLT + chunk, {"stn": dst})

        other_stations(send_volt)
    pack(wide_resp, resp_send, stn, range(pairs))
    resp_recv[stn] = resp_send[stn]
    pack(wide_volt, volt_send, stn, range(pairs))
    volt_recv[stn] = volt_send[stn]

    loads[3].wait()
    flag = flags[...].astype(jnp.float32)
    mutual = (flag * flag.T).astype(jnp.bfloat16)
    wait_all(id_rows, n - 1, recv_sem.at[IDS])
    all_ids = jnp.sum(id_rows[...], axis=0)
    row = lax.broadcasted_iota(jnp.int32, (everyone, everyone), 0)
    column = lax.broadcasted_iota(jnp.int32, (everyone, everyone), 1)
    one_hot = (row == all_ids).astype(jnp.float32).astype(jnp.bfloat16)
    picked = dot(mutual, one_hot).T.astype(jnp.bfloat16)
    weight[...] = jnp.where(row == column, 0.0, dot(picked, one_hot))

    def unpack(recv, pair):
        block = recv[:, pl.ds(2 * pair * stations, 2 * stations), :].astype(jnp.float32)
        block = block.reshape(n, 2, stations, width)
        return [block[:, j].reshape(everyone, width) for j in range(2)]

    sign = jnp.where(lax.broadcasted_iota(jnp.int32, (1, width), 1) < half, -1.0, 1.0)
    loads[4].wait()
    loads[5].wait()
    steps = steps_ref[...].reshape(1, half)
    steps = jnp.concatenate([steps, steps], axis=1)

    def predict(t, gain_both, gain_turn):
        a = a_float[t]
        turned = gain_both * a + gain_turn * a_swap[t]
        applied[t, pl.ds(0, everyone), :] = turned.astype(jnp.bfloat16)
        applied[t, pl.ds(everyone, everyone), :] = (sign * pltpu.roll(turned, half, 1)).astype(jnp.bfloat16)
        return dot_last(applied[t, pl.ds(0, everyone), :], applied[t])

    def gain_parts(gain):
        swapped = pltpu.roll(gain, half, 1)
        left = sign < 0.0
        return jnp.where(left, gain, swapped), jnp.where(left, -swapped, gain)

    wait_all(resp_recv, n - 1, recv_sem.at[RESP])
    gain_both, gain_turn = gain_parts(gains[...])
    for pair in range(spd // 2):
        for j, a in enumerate(unpack(resp_recv, pair)):
            t = 2 * pair + j
            a_float[t] = a
            a_swap[t] = pltpu.roll(a, half, 1)
            predicted[t] = predict(t, gain_both, gain_turn)

    def accumulate(t, left_over, totals):
        residual = jnp.concatenate(
            [
                (weight[...] * left_over[:, :everyone]).astype(jnp.bfloat16),
                (weight[...] * left_over[:, everyone:]).astype(jnp.bfloat16),
            ],
            axis=1,
        )
        hidden = dot(residual, applied[t])
        return totals[0] + a_float[t] * hidden, totals[1] + a_swap[t] * hidden

    def volt_chunk(chunk):
        part = volt_recv.at[pl.ds(0, n - 1), chunk_rows[chunk]]
        return pltpu.make_async_copy(part, part, recv_sem.at[VOLT + chunk])

    for iteration in range(ITERS):
        totals = (jnp.zeros((everyone, width), jnp.float32), jnp.zeros((everyone, width), jnp.float32))
        if iteration == 0:
            for chunk in range(chunks):
                volt_chunk(chunk).wait()
                for pair in chunk_pairs[chunk]:
                    for j, x in enumerate(unpack(volt_recv, pair)):
                        t = 2 * pair + j
                        mine = x.astype(jnp.bfloat16)
                        turned = (sign * pltpu.roll(x, half, 1)).astype(jnp.bfloat16)
                        seen = dot_last(mine, jnp.concatenate([mine, turned], axis=0))
                        observed[t] = seen
                        totals = accumulate(t, seen - predicted[t], totals)
        else:
            gain_both, gain_turn = gain_parts(current[...])
            left_over = observed[0] - predict(0, gain_both, gain_turn)
            for t in range(spd):
                held_over = left_over
                if t + 1 < spd:
                    left_over = observed[t + 1] - predict(t + 1, gain_both, gain_turn)
                totals = accumulate(t, held_over, totals)
        direct, crossed = totals
        energy = jnp.where(
            sign < 0.0,
            direct + pltpu.roll(direct, half, 1),
            crossed - pltpu.roll(crossed, half, 1),
        )
        energies[iteration, chan] = energy.reshape(n, stations, width)
        mine = energies.at[iteration, chan]
        other_chans(lambda c: remote(mine, mine, PAIR + iteration, {"chan": c}))
        wait_all(energies.at[iteration], nchan - 1, recv_sem.at[PAIR + iteration])
        chip_sum[iteration] = jnp.sum(energies[iteration], axis=0)
        other_stations(
            lambda s: remote(
                chip_sum.at[iteration, s], sums.at[iteration, stn], SUMS + iteration, {"stn": s}
            )
        )
        sums[iteration, stn] = chip_sum[iteration, stn]
        wait_all(sums.at[iteration], n - 1, recv_sem.at[SUMS + iteration])
        scale = -(2.0 / half) / half
        block = scale * jnp.sum(sums[iteration], axis=0)
        if iteration < ITERS - 1:
            gathered[iteration, stn] = block
            part = gathered.at[iteration, stn]
            other_stations(lambda s: remote(part, part, GATHER + iteration, {"stn": s}))
            wait_all(gathered.at[iteration], n - 1, recv_sem.at[GATHER + iteration])
            gradient = gathered[iteration].reshape(everyone, width)
            spread = jnp.sqrt(jnp.sum(gradient * gradient, keepdims=True) / (everyone * half) + 1e-06)
            held = gains if iteration == 0 else current
            current[...] = held[...] - steps * (gradient / spread)
        else:
            norms[stn] = jnp.sum(block * block, axis=0, keepdims=True)
            part = norms.at[stn]
            other_stations(lambda s: remote(part, part, GATHER + iteration, {"stn": s}))
            own = current[pl.ds(pl.multiple_of(stn * stations, stations), stations), :]
            wait_all(norms, n - 1, recv_sem.at[GATHER + iteration])
            total = jnp.sum(jnp.sum(norms[...], axis=0), keepdims=True)
            spread = jnp.sqrt(total / (everyone * half) + 1e-06)
            descent = block / spread
            result_ref[0] = own - steps * descent
            result_ref[1] = descent

    wait_all(id_rows, n - 1, send_sem.at[IDS])
    wait_all(resp_send, n - 1, send_sem.at[RESP])
    for chunk in range(chunks):
        part = volt_send.at[pl.ds(0, n - 1), chunk_rows[chunk]]
        pltpu.make_async_copy(part, part, send_sem.at[VOLT + chunk]).wait()
    for iteration in range(ITERS):
        wait_all(energies.at[iteration], nchan - 1, send_sem.at[PAIR + iteration])
        wait_all(sums.at[iteration], n - 1, send_sem.at[SUMS + iteration])
        last = gathered.at[iteration] if iteration < ITERS - 1 else norms
        wait_all(last, n - 1, send_sem.at[GATHER + iteration])


def shards(n, nchan, voltages, response, start_gains, step_sizes, station_ids, baseline_flags):
    stations, width = voltages.shape[0], voltages.shape[3]
    samples = voltages.shape[1] * voltages.shape[2]
    everyone = stations * n
    spd = samples // n
    half = width // 2
    f32, bf16 = jnp.float32, jnp.bfloat16
    hbm = pl.BlockSpec(memory_space=pltpu.HBM)
    vmem = pl.BlockSpec(memory_space=pltpu.VMEM)
    block = (n, spd * stations, width)
    scratch = [
        ((stations, samples, width), bf16),
        ((stations, samples, width), bf16),
        ((everyone, width), f32),
        ((everyone, everyone), jnp.int32),
        ((stations * (samples + 8), width), f32),
        ((stations * (samples + 8), width), f32),
        (block, bf16),
        (block, bf16),
        (block, bf16),
        (block, bf16),
        ((n, 1, everyone), jnp.int32),
        ((everyone, everyone), f32),
        ((spd, everyone, width), f32),
        ((spd, everyone, width), f32),
        ((spd, 2 * everyone, width), bf16),
        ((spd, everyone, 2 * everyone), f32),
        ((spd, everyone, 2 * everyone), f32),
        ((ITERS, nchan, n, stations, width), f32),
        ((ITERS, n, stations, width), f32),
        ((ITERS, n, stations, width), f32),
        ((ITERS - 1, n, stations, width), f32),
        ((n, 1, width), f32),
        ((everyone, width), f32),
        ((half,), f32),
    ]
    result = pl.pallas_call(
        functools.partial(kernel, n, nchan, stations, samples),
        out_shape=jax.ShapeDtypeStruct((2, stations, width), f32),
        in_specs=[hbm] * 6,
        out_specs=vmem,
        scratch_shapes=[pltpu.VMEM(shape, dtype) for shape, dtype in scratch]
        + [pltpu.SMEM((stations,), jnp.int32), pltpu.SemaphoreType.DMA((6,)), pltpu.SemaphoreType.DMA((GROUPS,)), pltpu.SemaphoreType.DMA((GROUPS,))],
        compiler_params=pltpu.CompilerParams(
            collective_id=0, has_side_effects=True, vmem_limit_bytes=64 * 1024 * 1024
        ),
    )(
        voltages.reshape(stations, samples, width),
        response.reshape(stations, samples, width),
        start_gains, step_sizes, station_ids, baseline_flags,
    )
    return result[0], result[1]


def solution(mesh):
    placed = (P("stn", "chan", None, None), P("stn", "chan", None, None), P(), P(), P("stn"), P())
    return jax.shard_map(
        functools.partial(shards, mesh.shape["stn"], mesh.shape["chan"]),
        mesh=mesh,
        in_specs=placed,
        out_specs=(P("stn", None), P("stn", None)),
        check_vma=False,
    )
```
